32 devices in a mesh: tm: 8 (over y, x, core), heads: 4 (over z).
Axes of the slice: x: 2, y: 2, z: 4, core: 2. Of those that a mesh axis runs over, the one named last changes fastest.
Arguments:
- layer_input: bfloat16 [1024, 8192], P('tm', 'heads'), may hold values from -0.119628906 to 0.119628906
- proj_weight: bfloat16 [512, 8192], P('tm', 'heads'), may hold values from -0.0625 to 0.0625
- ssd_input: float32 [1024, 2048], P('tm', 'heads'), may hold values from -0.036 to 0.036
- log_decay: float32 [1024, 32], P('tm', 'heads'), may hold values from -1 to 0, as said below
- out_grad: float32 [1024, 2048], P('tm', 'heads'), may hold values from -15 to 15
Outputs:
- grad_x: float32 [1024, 2048], P('tm', 'heads')
- grad_log: float32 [1024, 32], P('tm', 'heads')
- grad_input: bfloat16 [1024, 8192], P('tm', 'heads')
- grad_weight: float32 [512, 8192], P('tm', 'heads')
The draws below stay inside these ranges and needn't reach their ends.
Inputs may be any that keep to these rules, and one draw needn't show every extreme that they name: `log_decay`: all entries are negative.
All inputs are finite; a program needn't handle non-finite values.
Results may differ from the reference program's by a relative error of at most 0.023.
Values may be sent and summed in bfloat16 or wider, within the bound.
A program may use at most 64 MiB of HBM per device.

```python
import jax
import jax.numpy as jnp
from jax import lax

D = 8192
N = 128
P_SIZE = 64
SPAN = 128
TOK_DEV = 128
TOKEN_TOTAL = 1024
HEAD_TOTAL = 32
GROUPS = 2


def draw_log_decay(key, part):
    key = jax.random.fold_in(key, 7)
    random_keys = jax.random.split(key, 7)
    fast_share = 0.5
    fast = jax.random.bernoulli(random_keys[0], fast_share, (HEAD_TOTAL,))
    fast_rate = jnp.exp(jax.random.uniform(random_keys[1], (HEAD_TOTAL,), jnp.float32, jnp.log(1.0 / 50.0), jnp.log(1.0 / 30.0)))
    slow_rate = jnp.exp(jax.random.uniform(random_keys[2], (HEAD_TOTAL,), jnp.float32, jnp.log(0.01), jnp.log(0.05))) * 2.3 / TOKEN_TOTAL
    baseline_rate = jnp.where(fast, fast_rate, slow_rate)
    history_factor = jnp.exp(jax.random.uniform(random_keys[3], (TOKEN_TOTAL // TOK_DEV, HEAD_TOTAL), jnp.float32, jnp.log(0.5), jnp.log(2.0)))
    history_factor = jnp.repeat(history_factor, TOK_DEV, axis=0)
    coarse_estimate = jax.random.uniform(random_keys[4], (TOKEN_TOTAL, HEAD_TOTAL), jnp.float32, 0.5, 1.5)
    spike_position = jax.random.randint(random_keys[5], (3, HEAD_TOTAL), 0, TOKEN_TOTAL)
    time_steps = jnp.arange(TOKEN_TOTAL)
    spike_mask = jnp.any(time_steps[:, None, None] == spike_position[None, :, :], axis=1)
    spike_logarithm = jnp.log(jax.random.uniform(random_keys[6], (TOKEN_TOTAL, HEAD_TOTAL), jnp.float32, 0.5, 0.8))
    value_rows = -baseline_rate[None, :] * history_factor * coarse_estimate + jnp.where(spike_mask, spike_logarithm, 0.0)
    return value_rows.astype(jnp.float32)


def levels(stream_key, dims, shards, low, top_value):
    def one(dim, shards_of):
        heights = jax.random.uniform(jax.random.fold_in(jax.random.fold_in(stream_key, 6), dim), (shards_of,), jnp.float32, low / len(shards), top_value / len(shards))
        return jnp.repeat(jnp.exp(heights), dims[dim] // shards_of).reshape((-1,) + (1,) * (len(dims) - dim - 1))

    gain = one(*shards[0])
    for cut in shards[1:]:
        gain = gain * one(*cut)
    return gain


def centred(rng, extent, width, most, cuts=(), dtype=jnp.bfloat16):
    drawn = jax.random.normal(rng, extent, jnp.float32) * width
    if len(cuts) > 0:
        drawn = levels(rng, extent, cuts, -0.22, 0.18) * drawn
    return jnp.clip(drawn, min=-most, max=most).astype(dtype)


def setup_inputs(seed: int = 0) -> dict:
    streams_of = jax.random.split(jax.random.key(seed), 6)
    layer_input = centred(streams_of[0], (TOKEN_TOTAL, D), 0.02, 0.119628906, ((0, 8), (1, 4)))
    proj_weight = centred(streams_of[1], (2 * GROUPS * N, D), D ** -0.5, 0.0625, ((0, 8), (1, 4)))
    ssd_input = centred(streams_of[2], (TOKEN_TOTAL, HEAD_TOTAL * P_SIZE), 0.006, 0.036, ((0, 8), (1, 4)), jnp.float32)
    log_decay = draw_log_decay(jax.random.fold_in(streams_of[5], 71), 0)
    out_grad = centred(streams_of[4], (TOKEN_TOTAL, HEAD_TOTAL * P_SIZE), 2.5, 15.0, ((0, 8), (1, 4)), jnp.float32)
    return {"layer_input": layer_input, "proj_weight": proj_weight, "ssd_input": ssd_input, "log_decay": log_decay, "out_grad": out_grad}


highest = lax.Precision.HIGHEST


def span_sums(inputs, out_grads, logs, b_rows, c_rows):
    positions = jnp.arange(inputs.shape[0])
    lower_ones = (positions[:, None] >= positions[None, :]).astype(jnp.float32)
    cumlog = jnp.dot(lower_ones, logs, precision=highest)
    decay_sum = cumlog[-1]
    head_state = jnp.einsum('jn,jh,jhp->hnp', b_rows, jnp.exp(decay_sum[None] - cumlog), inputs, precision=highest)
    grad_state = jnp.einsum('in,ih,ihp->hnp', c_rows, jnp.exp(cumlog), out_grads, precision=highest)
    return decay_sum, head_state, grad_state


def span_grads(inputs, out_grads, logs, b_rows, c_rows, state_in, grad_out):
    positions = jnp.arange(inputs.shape[0])
    causal = positions[:, None] >= positions[None, :]
    lower_ones = causal.astype(jnp.float32)
    strict_ones = (positions[:, None] < positions[None, :]).astype(jnp.float32)
    cumlog = jnp.dot(lower_ones, logs, precision=highest)
    decay_sum = cumlog[-1]
    log_gaps = cumlog.T[:, :, None] - cumlog.T[:, None, :]
    decay_mat = jnp.where(causal[None], jnp.exp(jnp.minimum(log_gaps, 0.0)), 0.0)
    inner_cb = jnp.dot(c_rows, b_rows.T, precision=highest)
    inner_gx = jnp.einsum('ihp,jhp->hij', out_grads, inputs, precision=highest)
    decayed_cb = decay_mat * inner_cb[None]
    decayed_gx = decay_mat * inner_gx
    to_end = jnp.exp(decay_sum[None] - cumlog)
    from_start = jnp.exp(cumlog)
    b_state = jnp.einsum('jn,hnp->jhp', b_rows, grad_out, precision=highest)
    c_state = jnp.einsum('in,hnp->ihp', c_rows, state_in, precision=highest)
    grad_in = jnp.einsum('hij,ihp->jhp', decayed_cb, out_grads, precision=highest) + to_end[:, :, None] * b_state
    x_state = jnp.einsum('jhp,hnp->jhn', inputs, grad_out, precision=highest)
    grad_b = jnp.einsum('hij,in->jn', decayed_gx, c_rows, precision=highest) + jnp.einsum('jh,jhn->jn', to_end, x_state, precision=highest)
    g_state = jnp.einsum('ihp,hnp->ihn', out_grads, state_in, precision=highest)
    grad_c = jnp.einsum('hij,jn->in', decayed_gx, b_rows, precision=highest) + jnp.einsum('ih,ihn->in', from_start, g_state, precision=highest)
    pair_weight = decayed_cb * inner_gx
    prefix_sum = jnp.einsum('hij,jt->hit', pair_weight, strict_ones, precision=highest)
    inside = jnp.einsum('it,hit->th', lower_ones, prefix_sum, precision=highest)
    earlier = from_start * jnp.sum(c_state * out_grads, axis=2)
    later_terms = to_end * jnp.sum(b_state * inputs, axis=2)
    across = jnp.sum(grad_out * state_in, axis=(1, 2)) * jnp.exp(decay_sum)
    grad_log = inside + jnp.dot(lower_ones.T, earlier, precision=highest) + jnp.dot(strict_ones.T, later_terms, precision=highest) + across[None]
    return grad_in, grad_log, grad_b, grad_c


def reference(layer_input, proj_weight, ssd_input, log_decay, out_grad):
    bc_full = jnp.dot(layer_input, proj_weight.T, preferred_element_type=jnp.float32)
    groups = bc_full.shape[1] // (2 * N)
    per_group = HEAD_TOTAL // groups
    spans = TOKEN_TOTAL // SPAN
    inputs = ssd_input.reshape(spans, SPAN, groups, per_group, P_SIZE)
    out_grads = out_grad.reshape(spans, SPAN, groups, per_group, P_SIZE)
    logs = log_decay.reshape(spans, SPAN, groups, per_group)
    split_bc = bc_full.reshape(spans, SPAN, groups, 2, N)
    b_rows = split_bc[:, :, :, 0]
    c_rows = split_bc[:, :, :, 1]
    sums_fn = jax.vmap(span_sums, in_axes=(1, 1, 1, 1, 1))
    grads_fn = jax.vmap(span_grads, in_axes=(1, 1, 1, 1, 1, 0, 0), out_axes=(1, 1, 1, 1))
    zero_state = jnp.zeros((groups, per_group, N, P_SIZE), jnp.float32)
    items = (inputs, out_grads, logs, b_rows, c_rows)

    def forward(carry, item):
        decay_sum, head_state, grad_state = sums_fn(*item)
        return jnp.exp(decay_sum)[:, :, None, None] * carry + head_state, carry

    def backward(carry, item):
        decay_sum, head_state, grad_state = sums_fn(*item)
        return jnp.exp(decay_sum)[:, :, None, None] * carry + grad_state, carry

    _, states = lax.scan(forward, zero_state, items)
    _, grads = lax.scan(backward, zero_state, items, reverse=True)
    results = lax.map(lambda item: grads_fn(*item), (inputs, out_grads, logs, b_rows, c_rows, states, grads))
    grad_x = results[0].reshape(TOKEN_TOTAL, HEAD_TOTAL * P_SIZE)
    grad_log = results[1].reshape(TOKEN_TOTAL, HEAD_TOTAL)
    grad_bc = jnp.stack([results[2], results[3]], axis=3).reshape(TOKEN_TOTAL, groups * 2 * N).astype(jnp.bfloat16)
    grad_input = jnp.dot(grad_bc, proj_weight, preferred_element_type=jnp.float32).astype(jnp.bfloat16)
    grad_weight = jnp.dot(grad_bc.T, layer_input, preferred_element_type=jnp.float32)
    return grad_x, grad_log, grad_input, grad_weight
```

```python
import jax
import jax.numpy as jnp
from jax import lax
from jax.experimental import pallas as pl
from jax.experimental.pallas import tpu as pltpu
from jax.sharding import PartitionSpec as P

N = 128
MESH = pl.DeviceIdType.MESH
HIGH = lax.Precision.HIGHEST
F32 = jnp.float32
BF16 = jnp.bfloat16


def nn(a, b, precision=None):
    return lax.dot_general(
        a, b, (((1,), (0,)), ((), ())), precision=precision, preferred_element_type=F32
    )


def nt(a, b, precision=None):
    return lax.dot_general(
        a, b, (((1,), (1,)), ((), ())), precision=precision, preferred_element_type=F32
    )


class Gather:
    def __init__(self, buf, send, recv, tm, me, heads_at):
        self.buf, self.send, self.recv = buf, send, recv
        self.tm, self.me, self.z = tm, me, heads_at
        self.chips = tm // 2
        self.chip, self.core = me // 2, lax.rem(me, 2)
        self.half_rows = buf.shape[1] // 2
        self.pending = []
        chip = self.chip
        if self.chips == 4:
            self.xn = chip + 1 - 2 * lax.rem(chip, 2)
            self.yn = lax.rem(chip + 2, 4)
            self.dg = 3 - chip

    def piece(self, slot, half):
        return self.buf.at[slot, pl.ds(half * self.half_rows, self.half_rows)]

    def copy(self, slot, half, chip, core, number):
        part = self.piece(slot, half)
        return pltpu.make_async_remote_copy(
            src_ref=part,
            dst_ref=part,
            send_sem=self.send.at[number],
            recv_sem=self.recv.at[slot, half],
            device_id=(chip * 2 + core, self.z),
            device_id_type=MESH,
        )

    def push(self, slot, half, chip, core):
        made = self.copy(slot, half, chip, core, len(self.pending))
        made.start()
        self.pending.append(made)

    def arrive(self, slot, half):
        self.copy(slot, half, self.chip, 1 - self.core, 0).wait_recv()

    def start(self):
        me, core = self.me, self.core
        if self.chips == 4:
            self.push(me, 0, self.xn, core)
            self.push(me, 1, self.yn, core)
            self.push(me, 1, self.xn, core)
            self.push(me, 0, self.yn, core)
        else:
            for d in range(1, self.chips):
                for half in range(2):
                    self.push(me, half, lax.rem(self.chip + d, self.chips), core)
        for half in range(2):
            self.push(me, half, self.chip, 1 - core)

    def near(self):
        core = self.core
        if self.chips == 4:
            xs, ys = self.xn * 2 + core, self.yn * 2 + core
            self.arrive(xs, 0)
            self.push(xs, 0, self.yn, core)
            self.arrive(ys, 1)
            self.push(ys, 1, self.xn, core)
            self.push(xs, 0, self.chip, 1 - core)
            self.push(ys, 1, self.chip, 1 - core)
            self.arrive(xs, 1)
            self.push(xs, 1, self.chip, 1 - core)
            self.arrive(ys, 0)
            self.push(ys, 0, self.chip, 1 - core)

    def far(self):
        core = self.core
        if self.chips == 4:
            slots = [self.dg * 2 + core]
        else:
            slots = [lax.rem(self.chip + d, self.chips) * 2 + core for d in range(1, self.chips)]
        for slot in slots:
            for half in range(2):
                self.arrive(slot, half)
                self.push(slot, half, self.chip, 1 - core)

    def other(self, chip):
        for half in range(2):
            self.arrive(chip * 2 + 1 - self.core, half)

    def finish(self):
        for made in self.pending:
            made.wait_send()


def exchange(src, dst, send, recv, count, me, place):
    copies = []
    for d in range(1, count):
        to = lax.rem(me + d, count)
        copies.append(
            pltpu.make_async_remote_copy(
                src_ref=src(d, to),
                dst_ref=dst.at[me],
                send_sem=send.at[d],
                recv_sem=recv.at[me],
                device_id=place(to),
                device_id_type=MESH,
            )
        )
    for made in copies:
        made.start()
    return copies


def landed(dst, send, recv, slot, to):
    return pltpu.make_async_remote_copy(
        src_ref=dst.at[slot],
        dst_ref=dst.at[slot],
        send_sem=send.at[0],
        recv_sem=recv.at[slot],
        device_id=to,
        device_id_type=MESH,
    )


def kernel(
    tm, heads, members,
    li_ref, w_ref, x_ref, log_ref, dy_ref,
    gx_ref, gl_ref, gi_ref, gw_ref,
    wbuf, libuf, dec, pbuf, bcr, st, strecv, hin, gout, decay, dgx, gbuf, grecv, gall, grow,
    w_send, w_recv, li_send, li_recv, d_send, d_recv, p_send, p_recv, s_send, s_recv,
    g_send, g_recv, a_send, a_recv,
):
    me = lax.axis_index("tm")
    z = lax.axis_index("heads")
    chips = tm // 2
    span = li_ref.shape[0]
    heads_here = log_ref.shape[1]
    width = x_ref.shape[1]
    size = width // heads_here
    rows_w = w_ref.shape[0]
    along = lambda to: (to, z)
    across_z = lambda to: (me, to)
    peer = (lax.rem(me + 1, tm), z)

    barrier = pltpu.get_barrier_semaphore()
    for d in range(1, tm):
        pl.semaphore_signal(
            barrier, inc=1, device_id=along(lax.rem(me + d, tm)), device_id_type=MESH
        )
    for d in range(1, heads):
        pl.semaphore_signal(
            barrier, inc=1, device_id=across_z(lax.rem(z + d, heads)), device_id_type=MESH
        )
    wbuf[me] = w_ref[...]
    libuf[me] = li_ref[...]
    pl.semaphore_wait(barrier, tm - 1 + heads - 1)

    weights = Gather(wbuf, w_send, w_recv, tm, me, z)
    layer = Gather(libuf, li_send, li_recv, tm, me, z)
    weights.start()
    started = []

    row = lax.broadcasted_iota(jnp.int32, (span, span), 0)
    col = lax.broadcasted_iota(jnp.int32, (span, span), 1)
    lower = (row >= col).astype(F32)
    upper = (row <= col).astype(F32)
    strict = (row > col).astype(F32)
    head_of = lax.broadcasted_iota(jnp.int32, (heads_here, width), 0) * size
    place = lax.broadcasted_iota(jnp.int32, (heads_here, width), 1)
    spread = ((place >= head_of) & (place < head_of + size)).astype(F32)
    logs = log_ref[...]
    sums = nn(lower, logs, HIGH)
    sums_t = sums.T
    wide = nn(lower, nn(logs, spread, HIGH), HIGH)
    total = wide[span - 1 : span, :]
    dec[me] = jnp.broadcast_to(total, (8, width))
    started += exchange(lambda d, to: dec.at[me], dec, d_send, d_recv, tm, me, along)
    from_start = jnp.exp(wide)
    to_end = jnp.exp(total - wide)
    x = x_ref[...]
    dy = dy_ref[...]
    x_end = (to_end * x).astype(BF16)
    dy_start = (from_start * dy).astype(BF16)
    x_half = x.astype(BF16)
    dy_half = dy.astype(BF16)

    dgx_sum = jnp.zeros((span, span), F32)
    for h in range(heads_here):
        cut = slice(h * size, (h + 1) * size)
        gaps = sums_t[h : h + 1, :] - sums[:, h : h + 1]
        step = jnp.where(row <= col, jnp.exp(jnp.minimum(gaps, 0.0)), 0.0)
        pairs = step * nt(x_half[:, cut], dy_half[:, cut])
        decay[h] = step
        dgx[h] = pairs
        dgx_sum = dgx_sum + pairs

    def project(chip):
        block = wbuf[pl.ds(2 * chip, 2)].reshape(2 * rows_w, wbuf.shape[2])
        pbuf[chip] = nt(li_ref[...], block).astype(BF16)

    weights.near()
    weights.other(weights.chip)
    project(weights.chip)
    if chips == 4:
        weights.other(weights.xn)
        project(weights.xn)
        weights.other(weights.yn)
        project(weights.yn)
        weights.far()
        weights.other(weights.dg)
        project(weights.dg)
    else:
        weights.far()
        for d in range(1, chips):
            chip = lax.rem(weights.chip + d, chips)
            weights.other(chip)
            project(chip)
    group = z // members
    bcr[z] = pbuf[pl.ds(2 * group, 2)]
    started += exchange(
        lambda d, to: pbuf.at[pl.ds(2 * (to // members), 2)], bcr, p_send, p_recv, heads, z, across_z
    )
    layer.start()
    for d in range(1, heads):
        landed(bcr, p_send, p_recv, lax.rem(z + d, heads), peer).wait_recv()
    bc = bcr[0].astype(F32)
    for k in range(1, heads):
        bc = bc + bcr[k].astype(F32)
    b_t = bc[0].T.astype(BF16)
    c_t = bc[1].T.astype(BF16)
    b = bc[0].astype(BF16)
    c = bc[1].astype(BF16)

    st[0] = nn(b_t, x_end).astype(BF16)
    st[1] = nn(c_t, dy_start).astype(BF16)
    started += exchange(
        lambda d, to: st.at[(me + d) // tm], strecv, s_send, s_recv, tm, me, along
    )

    cb = nt(b, c)
    after = []
    before = []
    for h in range(heads_here):
        cut = slice(h * size, (h + 1) * size)
        weight = decay[h] * cb
        gx_ref[:, cut] = nn(weight.astype(BF16), dy_half[:, cut])
        product = dgx[h] * cb
        after.append(jnp.sum(product, axis=1, keepdims=True))
        before.append(jnp.sum(product, axis=0, keepdims=True))
    before = jnp.concatenate(before, axis=0)
    after = jnp.concatenate(after, axis=1)
    grad_b = nn(c_t, dgx_sum.T.astype(BF16))
    grad_c = nn(b_t, dgx_sum.astype(BF16))
    inside = nn(strict, after, HIGH) - nt(strict, before, HIGH)

    hin[...] = jnp.zeros_like(hin)
    gout[...] = jnp.zeros_like(gout)

    def forward(q, _):
        landed(dec, d_send, d_recv, q, peer).wait_recv()
        landed(strecv, s_send, s_recv, q, peer).wait_recv()
        hin[...] = hin[...] * jnp.exp(dec[q][0:1, :]) + strecv[q].astype(F32)
        return 0

    def backward(k, _):
        q = tm - 1 - k
        landed(dec, d_send, d_recv, q, peer).wait_recv()
        landed(strecv, s_send, s_recv, q, peer).wait_recv()
        gout[...] = gout[...] * jnp.exp(dec[q][0:1, :]) + strecv[q].astype(F32)
        return 0

    lax.fori_loop(0, me, forward, 0)
    lax.fori_loop(0, tm - 1 - me, backward, 0)
    state = hin[...]
    grad = gout[...]
    state_half = state.astype(BF16)
    grad_half = grad.astype(BF16)
    gbuf[0] = (grad_b + nt(grad_half, x_end)).astype(BF16)
    gbuf[1] = (grad_c + nt(state_half, dy_start)).astype(BF16)
    grecv[z] = gbuf[...]
    started += exchange(lambda d, to: gbuf, grecv, g_send, g_recv, heads, z, across_z)

    from_end = to_end * nn(b, grad_half)
    gx_ref[...] += from_end
    earlier = nt(from_start * nn(c, state_half) * dy, spread, HIGH)
    later = nt(from_end * x, spread, HIGH)
    through = jnp.sum(grad * state, axis=0, keepdims=True) * jnp.exp(total)
    through = nt(jnp.broadcast_to(through, (8, width)), spread, HIGH)
    gl_ref[...] = (
        inside + nn(upper, earlier, HIGH) + nn(strict, later, HIGH) + through[0:1, :]
    )
    layer.near()

    for d in range(1, heads):
        landed(grecv, g_send, g_recv, lax.rem(z + d, heads), peer).wait_recv()
    turned = []
    for g in range(heads // members):
        for part in range(2):
            acc = grecv[g * members, part].astype(F32)
            for k in range(1, members):
                acc = acc + grecv[g * members + k, part].astype(F32)
            piece = acc.astype(BF16)
            first = (2 * g + part) * N // rows_w
            for k in range(N // rows_w):
                gall[first + k] = piece[k * rows_w : (k + 1) * rows_w]
            turned.append(piece.astype(F32).T.astype(BF16))
    started += exchange(lambda d, to: gall.at[to], grow, a_send, a_recv, tm, me, along)
    grow[me] = gall[me]
    layer.far()
    grad_bc = jnp.concatenate(turned, axis=1)
    gi_ref[...] = nn(grad_bc, wbuf[...].reshape(tm * rows_w, wbuf.shape[2])).astype(BF16)

    layer.other(layer.chip)
    for d in range(1, chips):
        layer.other(lax.rem(layer.chip + d, chips))
    for d in range(1, tm):
        landed(grow, a_send, a_recv, lax.rem(me + d, tm), peer).wait_recv()
    rows = jnp.concatenate([grow[k] for k in range(tm)], axis=1)
    gw_ref[...] = nn(rows, libuf[...].reshape(tm * span, libuf.shape[2]))

    for made in started:
        made.wait_send()
    weights.finish()
    layer.finish()


def solution(mesh):
    tm = mesh.shape["tm"]
    heads = mesh.shape["heads"]
    chips = tm // 2

    def on_device(layer_input, proj_weight, ssd_input, log_decay, out_grad):
        span, depth = layer_input.shape
        rows_w = proj_weight.shape[0]
        heads_here = log_decay.shape[1]
        width = ssd_input.shape[1]
        groups = rows_w * tm // (2 * N)
        members = heads // groups
        copies = 14 if chips == 4 else 4 * (chips - 1) + 2
        dma = lambda *shape: pltpu.SemaphoreType.DMA(shape)
        vmem = pl.BlockSpec(memory_space=pltpu.VMEM)

        def body(*refs):
            kernel(tm, heads, members, *refs)

        return pl.pallas_call(
            body,
            out_shape=(
                jax.ShapeDtypeStruct((span, width), F32),
                jax.ShapeDtypeStruct((span, heads_here), F32),
                jax.ShapeDtypeStruct((span, depth), BF16),
                jax.ShapeDtypeStruct((rows_w, depth), F32),
            ),
            in_specs=[vmem] * 5,
            out_specs=(vmem,) * 4,
            scratch_shapes=[
                pltpu.VMEM((tm, rows_w, depth), BF16),
                pltpu.VMEM((tm, span, depth), BF16),
                pltpu.VMEM((tm, 8, width), F32),
                pltpu.VMEM((chips, span, N), BF16),
                pltpu.VMEM((heads, 2, span, N), BF16),
                pltpu.VMEM((2, N, width), BF16),
                pltpu.VMEM((tm, N, width), BF16),
                pltpu.VMEM((N, width), F32),
                pltpu.VMEM((N, width), F32),
                pltpu.VMEM((heads_here, span, span), F32),
                pltpu.VMEM((heads_here, span, span), F32),
                pltpu.VMEM((2, N, span), BF16),
                pltpu.VMEM((heads, 2, N, span), BF16),
                pltpu.VMEM((tm, rows_w, span), BF16),
                pltpu.VMEM((tm, rows_w, span), BF16),
                dma(copies), dma(tm, 2),
                dma(copies), dma(tm, 2),
                dma(tm), dma(tm),
                dma(heads), dma(heads),
                dma(tm), dma(tm),
                dma(heads), dma(heads),
                dma(tm), dma(tm),
            ],
            compiler_params=pltpu.CompilerParams(
                collective_id=0, has_side_effects=True, vmem_limit_bytes=48 * 1024 * 1024
            ),
        )(layer_input, proj_weight, ssd_input, log_decay, out_grad)

    return jax.shard_map(
        on_device,
        mesh=mesh,
        in_specs=(P("tm", "heads"),) * 5,
        out_specs=(P("tm", "heads"),) * 4,
        check_vma=False,
    )
```

```python
import jax
import jax.numpy as jnp
from jax import lax
from jax.experimental import pallas as pl
from jax.experimental.pallas import tpu as pltpu
from jax.sharding import PartitionSpec as P

N = 128
MESH = pl.DeviceIdType.MESH
HIGH = lax.Precision.HIGHEST
F32 = jnp.float32
BF16 = jnp.bfloat16


def nn(a, b, precision=None):
    return lax.dot_general(
        a, b, (((1,), (0,)), ((), ())), precision=precision, preferred_element_type=F32
    )


def nt(a, b, precision=None):
    return lax.dot_general(
        a, b, (((1,), (1,)), ((), ())), precision=precision, preferred_element_type=F32
    )


class Gather:
    def __init__(self, buf, send, recv, tm, me, heads_at):
        self.buf, self.send, self.recv = buf, send, recv
        self.tm, self.me, self.z = tm, me, heads_at
        self.chips = tm // 2
        self.chip, self.core = me // 2, lax.rem(me, 2)
        self.half_rows = buf.shape[1] // 2
        self.pending = []
        chip = self.chip
        if self.chips == 4:
            self.xn = chip + 1 - 2 * lax.rem(chip, 2)
            self.yn = lax.rem(chip + 2, 4)
            self.dg = 3 - chip

    def piece(self, slot, half):
        return self.buf.at[slot, pl.ds(half * self.half_rows, self.half_rows)]

    def copy(self, slot, half, chip, core, number):
        part = self.piece(slot, half)
        return pltpu.make_async_remote_copy(
            src_ref=part,
            dst_ref=part,
            send_sem=self.send.at[number],
            recv_sem=self.recv.at[slot, half],
            device_id=(chip * 2 + core, self.z),
            device_id_type=MESH,
        )

    def push(self, slot, half, chip, core):
        made = self.copy(slot, half, chip, core, len(self.pending))
        made.start()
        self.pending.append(made)

    def arrive(self, slot, half):
        self.copy(slot, half, self.chip, 1 - self.core, 0).wait_recv()

    def start(self):
        self.first()
        self.second()

    def first(self):
        me, core = self.me, self.core
        if self.chips == 4:
            self.push(me, 0, self.xn, core)
            self.push(me, 1, self.yn, core)
        else:
            for d in range(1, self.chips):
                self.push(me, 0, lax.rem(self.chip + d, self.chips), core)
        for half in range(2):
            self.push(me, half, self.chip, 1 - core)

    def second(self):
        me, core = self.me, self.core
        if self.chips == 4:
            self.push(me, 1, self.xn, core)
            self.push(me, 0, self.yn, core)
        else:
            for d in range(1, self.chips):
                self.push(me, 1, lax.rem(self.chip + d, self.chips), core)

    def relay(self):
        core = self.core
        if self.chips == 4:
            xs, ys = self.xn * 2 + core, self.yn * 2 + core
            self.arrive(xs, 0)
            self.push(xs, 0, self.yn, core)
            self.arrive(ys, 1)
            self.push(ys, 1, self.xn, core)
            self.push(xs, 0, self.chip, 1 - core)
            self.push(ys, 1, self.chip, 1 - core)

    def near(self):
        core = self.core
        if self.chips == 4:
            xs, ys = self.xn * 2 + core, self.yn * 2 + core
            self.arrive(xs, 1)
            self.push(xs, 1, self.chip, 1 - core)
            self.arrive(ys, 0)
            self.push(ys, 0, self.chip, 1 - core)

    def far(self):
        core = self.core
        if self.chips == 4:
            slots = [self.dg * 2 + core]
        else:
            slots = [lax.rem(self.chip + d, self.chips) * 2 + core for d in range(1, self.chips)]
        for slot in slots:
            for half in range(2):
                self.arrive(slot, half)
                self.push(slot, half, self.chip, 1 - core)

    def other(self, chip):
        for half in range(2):
            self.arrive(chip * 2 + 1 - self.core, half)

    def finish(self):
        for made in self.pending:
            made.wait_send()


def exchange(src, dst, send, recv, count, me, place):
    copies = []
    for d in range(1, count):
        to = lax.rem(me + d, count)
        copies.append(
            pltpu.make_async_remote_copy(
                src_ref=src(d, to),
                dst_ref=dst.at[me],
                send_sem=send.at[d],
                recv_sem=recv.at[me],
                device_id=place(to),
                device_id_type=MESH,
            )
        )
    for made in copies:
        made.start()
    return copies


def landed(dst, send, recv, slot, to):
    return pltpu.make_async_remote_copy(
        src_ref=dst.at[slot],
        dst_ref=dst.at[slot],
        send_sem=send.at[0],
        recv_sem=recv.at[slot],
        device_id=to,
        device_id_type=MESH,
    )


def kernel(
    tm, heads, members,
    li_hbm, w_hbm, x_hbm, log_hbm, dy_hbm,
    gx_ref, gl_ref, gi_ref, gw_ref,
    x_ref, dy_ref, log_ref,
    wbuf, libuf, dec, pbuf, bcr, st, strecv, hin, gout, decay, dgx, gbuf, grecv, gall, grow,
    w_send, w_recv, li_send, li_recv, d_send, d_recv, p_send, p_recv, s_send, s_recv,
    g_send, g_recv, a_send, a_recv, in_sem,
):
    me = lax.axis_index("tm")
    z = lax.axis_index("heads")
    chips = tm // 2
    span = li_hbm.shape[0]
    heads_here = log_ref.shape[0]
    width = x_ref.shape[1]
    size = width // heads_here
    rows_w = w_hbm.shape[0]
    along = lambda to: (to, z)
    across_z = lambda to: (me, to)
    peer = (lax.rem(me + 1, tm), z)

    loads = [
        pltpu.make_async_copy(src, dst, in_sem.at[k])
        for k, (src, dst) in enumerate((
            (log_hbm, log_ref), (w_hbm, wbuf.at[me]), (x_hbm, x_ref), (dy_hbm, dy_ref),
            (li_hbm, libuf.at[me]),
        ))
    ]
    for made in loads:
        made.start()
    barrier = pltpu.get_barrier_semaphore()
    for d in range(1, tm):
        pl.semaphore_signal(
            barrier, inc=1, device_id=along(lax.rem(me + d, tm)), device_id_type=MESH
        )
    for d in range(1, heads):
        pl.semaphore_signal(
            barrier, inc=1, device_id=across_z(lax.rem(z + d, heads)), device_id_type=MESH
        )

    weights = Gather(wbuf, w_send, w_recv, tm, me, z)
    layer = Gather(libuf, li_send, li_recv, tm, me, z)
    started = []

    row = lax.broadcasted_iota(jnp.int32, (span, span), 0)
    col = lax.broadcasted_iota(jnp.int32, (span, span), 1)
    lower = (row >= col).astype(F32)
    upper = (row <= col).astype(F32)
    strict = (row > col).astype(F32)
    head_of = lax.broadcasted_iota(jnp.int32, (heads_here, width), 0) * size
    place = lax.broadcasted_iota(jnp.int32, (heads_here, width), 1)
    spread = ((place >= head_of) & (place < head_of + size)).astype(F32)
    loads[0].wait()
    sums_t = nn(log_ref[...], upper, HIGH)
    sums = sums_t.T
    wide = nn(sums, spread, HIGH)
    total = wide[span - 1 : span, :]
    dec[me] = jnp.broadcast_to(total, (8, width))
    loads[1].wait()
    pl.semaphore_wait(barrier, tm - 1 + heads - 1)
    weights.start()
    started += exchange(lambda d, to: dec.at[me], dec, d_send, d_recv, tm, me, along)
    loads[2].wait()
    loads[3].wait()
    from_start = jnp.exp(wide)
    to_end = jnp.exp(total - wide)
    x = x_ref[...]
    dy = dy_ref[...]
    x_end = (to_end * x).astype(BF16)
    dy_start = (from_start * dy).astype(BF16)
    x_half = x.astype(BF16)
    dy_half = dy.astype(BF16)

    weights.relay()

    dgx_sum = jnp.zeros((span, span), F32)
    for h in range(heads_here):
        cut = slice(h * size, (h + 1) * size)
        gaps = sums_t[h : h + 1, :] - sums[:, h : h + 1]
        step = jnp.where(row <= col, jnp.exp(jnp.minimum(gaps, 0.0)), 0.0)
        pairs = step * nt(x_half[:, cut], dy_half[:, cut])
        decay[h] = step
        dgx[h] = pairs
        dgx_sum = dgx_sum + pairs

    loads[4].wait()
    sent = []

    def project(chip):
        number = len(sent)
        block = wbuf[pl.ds(2 * chip, 2)].reshape(2 * rows_w, wbuf.shape[2])
        pbuf[chip] = nt(libuf[me], block).astype(BF16)
        part = lax.rem(chip, 2)
        made = []
        for m in range(members):
            to = chip // 2 * members + m
            made.append((to, pltpu.make_async_remote_copy(
                src_ref=pbuf.at[chip],
                dst_ref=bcr.at[z, part],
                send_sem=p_send.at[number, m],
                recv_sem=p_recv.at[z, part],
                device_id=across_z(to),
                device_id_type=MESH,
            )))
        sent.append(made)
        for to, copy in made:
            pl.when(to != z)(copy.start)

    weights.near()
    weights.other(weights.chip)
    project(weights.chip)
    if chips == 4:
        weights.other(weights.xn)
        project(weights.xn)
        weights.other(weights.yn)
        project(weights.yn)
        weights.far()
        layer.first()
        weights.other(weights.dg)
        project(weights.dg)
    else:
        weights.far()
        layer.first()
        for d in range(1, chips):
            chip = lax.rem(weights.chip + d, chips)
            weights.other(chip)
            project(chip)
    group = z // members
    bcr[z] = pbuf[pl.ds(2 * group, 2)]
    for d in range(1, heads):
        other = lax.rem(z + d, heads)
        for part in range(2):
            pltpu.make_async_remote_copy(
                src_ref=bcr.at[other, part],
                dst_ref=bcr.at[other, part],
                send_sem=p_send.at[0, 0],
                recv_sem=p_recv.at[other, part],
                device_id=peer,
                device_id_type=MESH,
            ).wait_recv()
    bc = bcr[0].astype(F32)
    for k in range(1, heads):
        bc = bc + bcr[k].astype(F32)
    b_t = bc[0].T.astype(BF16)
    c_t = bc[1].T.astype(BF16)
    b = bc[0].astype(BF16)
    c = bc[1].astype(BF16)

    st[0] = nn(b_t, x_end).astype(BF16)
    st[1] = nn(c_t, dy_start).astype(BF16)
    chip, core = me // 2, lax.rem(me, 2)

    def state_copy(src, slot, to, number):
        made = pltpu.make_async_remote_copy(
            src_ref=src,
            dst_ref=strecv.at[slot],
            send_sem=s_send.at[number],
            recv_sem=s_recv.at[slot],
            device_id=along(to),
            device_id_type=MESH,
        )
        made.start()
        return made

    for d in range(1, chips):
        to = lax.rem(chip + d, chips) * 2 + core
        started.append(state_copy(st.at[(chip + d) // chips], me, to, d))
    started.append(state_copy(st.at[core], me, chip * 2 + 1 - core, 0))

    cb = nt(b, c)
    after = []
    before = []
    for h in range(heads_here):
        cut = slice(h * size, (h + 1) * size)
        weight = decay[h] * cb
        gx_ref[:, cut] = nn(weight.astype(BF16), dy_half[:, cut])
        product = dgx[h] * cb
        after.append(jnp.sum(product, axis=1, keepdims=True))
        before.append(jnp.sum(product, axis=0, keepdims=True))
    before = jnp.concatenate(before, axis=0)
    after = jnp.concatenate(after, axis=1)
    grad_b = nn(c_t, dgx_sum.T.astype(BF16))
    grad_c = nn(b_t, dgx_sum.astype(BF16))
    inside = nn(strict, after, HIGH) - nt(strict, before, HIGH)

    for d in range(1, chips):
        slot = lax.rem(chip + d, chips) * 2 + core
        landed(strecv, s_send, s_recv, slot, peer).wait_recv()
        started.append(
            state_copy(strecv.at[slot], slot, chip * 2 + 1 - core, chips - 1 + d)
        )
    layer.second()
    layer.relay()
    for d in range(1, tm):
        landed(dec, d_send, d_recv, lax.rem(me + d, tm), peer).wait_recv()
    for d in range(chips):
        slot = lax.rem(chip + d, chips) * 2 + 1 - core
        landed(strecv, s_send, s_recv, slot, peer).wait_recv()
    hin[...] = jnp.zeros_like(hin)
    gout[...] = jnp.zeros_like(gout)

    def forward(q, _):
        hin[...] = hin[...] * jnp.exp(dec[q][0:1, :]) + strecv[q].astype(F32)
        return 0

    def backward(k, _):
        q = tm - 1 - k
        gout[...] = gout[...] * jnp.exp(dec[q][0:1, :]) + strecv[q].astype(F32)
        return 0

    lax.fori_loop(0, me, forward, 0)
    lax.fori_loop(0, tm - 1 - me, backward, 0)
    state = hin[...]
    grad = gout[...]
    state_half = state.astype(BF16)
    grad_half = grad.astype(BF16)
    gbuf[0] = (grad_b + nt(grad_half, x_end)).astype(BF16)
    gbuf[1] = (grad_c + nt(state_half, dy_start)).astype(BF16)
    grecv[z] = gbuf[...]
    started += exchange(lambda d, to: gbuf, grecv, g_send, g_recv, heads, z, across_z)

    from_end = to_end * nn(b, grad_half)
    gx_ref[...] += from_end
    earlier = nt(from_start * nn(c, state_half) * dy, spread, HIGH)
    later = nt(from_end * x, spread, HIGH)
    through = jnp.sum(grad * state, axis=0, keepdims=True) * jnp.exp(total)
    through = nt(jnp.broadcast_to(through, (8, width)), spread, HIGH)
    gl_ref[...] = (
        inside + nn(upper, earlier, HIGH) + nn(strict, later, HIGH) + through[0:1, :]
    ).T

    for d in range(1, heads):
        landed(grecv, g_send, g_recv, lax.rem(z + d, heads), peer).wait_recv()
    turned = []
    for g in range(heads // members):
        for part in range(2):
            acc = grecv[g * members, part].astype(F32)
            for k in range(1, members):
                acc = acc + grecv[g * members + k, part].astype(F32)
            piece = acc.astype(BF16)
            first = (2 * g + part) * N // rows_w
            for k in range(N // rows_w):
                gall[first + k] = piece[k * rows_w : (k + 1) * rows_w]
            turned.append(piece.astype(F32).T.astype(BF16))
    started += exchange(lambda d, to: gall.at[to], grow, a_send, a_recv, tm, me, along)
    grow[me] = gall[me]
    layer.near()
    layer.far()
    grad_bc = jnp.concatenate(turned, axis=1)
    gi_ref[...] = nn(grad_bc, wbuf[...].reshape(tm * rows_w, wbuf.shape[2])).astype(BF16)

    layer.other(layer.chip)
    for d in range(1, chips):
        layer.other(lax.rem(layer.chip + d, chips))
    for d in range(1, tm):
        landed(grow, a_send, a_recv, lax.rem(me + d, tm), peer).wait_recv()
    rows = jnp.concatenate([grow[k] for k in range(tm)], axis=1)
    gw_ref[...] = nn(rows, libuf[...].reshape(tm * span, libuf.shape[2]))

    for made in started:
        made.wait_send()
    for made in sent:
        for to, copy in made:
            pl.when(to != z)(copy.wait_send)
    weights.finish()
    layer.finish()


def store(*refs):
    sems = refs[-1]
    count = (len(refs) - 1) // 2
    copies = [pltpu.make_async_copy(refs[k], refs[count + k], sems.at[k]) for k in range(count)]
    for made in copies:
        made.start()
    for made in copies:
        made.wait()


def solution(mesh):
    tm = mesh.shape["tm"]
    heads = mesh.shape["heads"]
    chips = tm // 2

    def on_device(layer_input, proj_weight, ssd_input, log_decay, out_grad):
        span, depth = layer_input.shape
        rows_w = proj_weight.shape[0]
        heads_here = log_decay.shape[1]
        width = ssd_input.shape[1]
        groups = rows_w * tm // (2 * N)
        members = heads // groups
        copies = 14 if chips == 4 else 4 * (chips - 1) + 2
        dma = lambda *shape: pltpu.SemaphoreType.DMA(shape)
        vmem = pl.BlockSpec(memory_space=pltpu.VMEM)
        hbm = pl.BlockSpec(memory_space=pltpu.HBM)
        shapes = (
            jax.ShapeDtypeStruct((span, width), F32),
            jax.ShapeDtypeStruct((heads_here, span), F32),
            jax.ShapeDtypeStruct((span, depth), BF16),
            jax.ShapeDtypeStruct((rows_w, depth), F32),
        )

        def body(*refs):
            kernel(tm, heads, members, *refs)

        results = pl.pallas_call(
            body,
            out_shape=tuple(pltpu.VMEM(k.shape, k.dtype) for k in shapes),
            in_specs=[hbm] * 5,
            out_specs=(vmem,) * 4,
            scratch_shapes=[
                pltpu.VMEM((span, width), F32),
                pltpu.VMEM((span, width), F32),
                pltpu.VMEM((heads_here, span), F32),
                pltpu.VMEM((tm, rows_w, depth), BF16),
                pltpu.VMEM((tm, span, depth), BF16),
                pltpu.VMEM((tm, 8, width), F32),
                pltpu.VMEM((chips, span, N), BF16),
                pltpu.VMEM((heads, 2, span, N), BF16),
                pltpu.VMEM((2, N, width), BF16),
                pltpu.VMEM((tm, N, width), BF16),
                pltpu.VMEM((N, width), F32),
                pltpu.VMEM((N, width), F32),
                pltpu.VMEM((heads_here, span, span), F32),
                pltpu.VMEM((heads_here, span, span), F32),
                pltpu.VMEM((2, N, span), BF16),
                pltpu.VMEM((heads, 2, N, span), BF16),
                pltpu.VMEM((tm, rows_w, span), BF16),
                pltpu.VMEM((tm, rows_w, span), BF16),
                dma(copies), dma(tm, 2),
                dma(copies), dma(tm, 2),
                dma(tm), dma(tm),
                dma(chips, members), dma(heads, 2),
                dma(tm), dma(tm),
                dma(heads), dma(heads),
                dma(tm), dma(tm),
                dma(5),
            ],
            compiler_params=pltpu.CompilerParams(
                collective_id=0, has_side_effects=True, vmem_limit_bytes=56 * 1024 * 1024
            ),
        )(layer_input, proj_weight, ssd_input, log_decay.T, out_grad)
        grad_x, grad_log, grad_input, grad_weight = pl.pallas_call(
            store,
            out_shape=shapes,
            in_specs=[vmem] * 4,
            out_specs=(hbm,) * 4,
            scratch_shapes=[dma(4)],
        )(*results)
        return grad_x, grad_log.T, grad_input, grad_weight

    return jax.shard_map(
        on_device,
        mesh=mesh,
        in_specs=(P("tm", "heads"),) * 5,
        out_specs=(P("tm", "heads"),) * 4,
        check_vma=False,
    )
```

```python
import jax
import jax.numpy as jnp
from jax import lax
from jax.experimental import pallas as pl
from jax.experimental.pallas import tpu as pltpu
from jax.sharding import PartitionSpec as P

N = 128
MESH = pl.DeviceIdType.MESH
HIGH = lax.Precision.HIGHEST
F32 = jnp.float32
BF16 = jnp.bfloat16


def nn(a, b, precision=None):
    return lax.dot_general(
        a, b, (((1,), (0,)), ((), ())), precision=precision, preferred_element_type=F32
    )


def nt(a, b, precision=None):
    return lax.dot_general(
        a, b, (((1,), (1,)), ((), ())), precision=precision, preferred_element_type=F32
    )


class Gather:
    def __init__(self, buf, send, recv, tm, me, heads_at):
        self.buf, self.send, self.recv = buf, send, recv
        self.tm, self.me, self.z = tm, me, heads_at
        self.chips = tm // 2
        self.chip, self.core = me // 2, lax.rem(me, 2)
        self.half_rows = buf.shape[1] // 2
        self.pending = []
        chip = self.chip
        if self.chips == 4:
            self.xn = chip + 1 - 2 * lax.rem(chip, 2)
            self.yn = lax.rem(chip + 2, 4)
            self.dg = 3 - chip

    def piece(self, slot, half):
        return self.buf.at[slot, pl.ds(half * self.half_rows, self.half_rows)]

    def copy(self, slot, half, chip, core, number):
        part = self.piece(slot, half)
        return pltpu.make_async_remote_copy(
            src_ref=part,
            dst_ref=part,
            send_sem=self.send.at[number],
            recv_sem=self.recv.at[slot, half],
            device_id=(chip * 2 + core, self.z),
            device_id_type=MESH,
        )

    def push(self, slot, half, chip, core):
        made = self.copy(slot, half, chip, core, len(self.pending))
        made.start()
        self.pending.append(made)

    def arrive(self, slot, half):
        self.copy(slot, half, self.chip, 1 - self.core, 0).wait_recv()

    def start(self):
        self.first()
        self.second()

    def first(self):
        me, core = self.me, self.core
        if self.chips == 4:
            self.push(me, 0, self.xn, core)
            self.push(me, 1, self.yn, core)
        else:
            for d in range(1, self.chips):
                self.push(me, 0, lax.rem(self.chip + d, self.chips), core)
        for half in range(2):
            self.push(me, half, self.chip, 1 - core)

    def second(self):
        me, core = self.me, self.core
        if self.chips == 4:
            self.push(me, 1, self.xn, core)
            self.push(me, 0, self.yn, core)
        else:
            for d in range(1, self.chips):
                self.push(me, 1, lax.rem(self.chip + d, self.chips), core)

    def relay(self):
        core = self.core
        if self.chips == 4:
            xs, ys = self.xn * 2 + core, self.yn * 2 + core
            self.arrive(xs, 0)
            self.push(xs, 0, self.yn, core)
            self.arrive(ys, 1)
            self.push(ys, 1, self.xn, core)
            self.push(xs, 0, self.chip, 1 - core)
            self.push(ys, 1, self.chip, 1 - core)

    def near(self):
        core = self.core
        if self.chips == 4:
            xs, ys = self.xn * 2 + core, self.yn * 2 + core
            self.arrive(xs, 1)
            self.push(xs, 1, self.chip, 1 - core)
            self.arrive(ys, 0)
            self.push(ys, 0, self.chip, 1 - core)

    def far(self):
        core = self.core
        if self.chips == 4:
            slots = [self.dg * 2 + core]
        else:
            slots = [lax.rem(self.chip + d, self.chips) * 2 + core for d in range(1, self.chips)]
        for slot in slots:
            for half in range(2):
                self.arrive(slot, half)
                self.push(slot, half, self.chip, 1 - core)

    def other(self, chip):
        for half in range(2):
            self.arrive(chip * 2 + 1 - self.core, half)

    def finish(self):
        for made in self.pending:
            made.wait_send()


def exchange(src, dst, send, recv, count, me, place):
    copies = []
    for d in range(1, count):
        to = lax.rem(me + d, count)
        copies.append(
            pltpu.make_async_remote_copy(
                src_ref=src(d, to),
                dst_ref=dst.at[me],
                send_sem=send.at[d],
                recv_sem=recv.at[me],
                device_id=place(to),
                device_id_type=MESH,
            )
        )
    for made in copies:
        made.start()
    return copies


def landed(dst, send, recv, slot, to):
    return pltpu.make_async_remote_copy(
        src_ref=dst.at[slot],
        dst_ref=dst.at[slot],
        send_sem=send.at[0],
        recv_sem=recv.at[slot],
        device_id=to,
        device_id_type=MESH,
    )


def kernel(
    tm, heads, members,
    li_hbm, w_hbm, x_hbm, log_hbm, dy_hbm,
    gx_ref, gl_ref, gi_ref, gw_ref,
    x_ref, dy_ref, log_ref,
    wbuf, libuf, dec, pbuf, bcr, st, strecv, hin, gout, decay, dgx, gbuf, grecv, gall, grow,
    w_send, w_recv, li_send, li_recv, d_send, d_recv, p_send, p_recv, s_send, s_recv,
    g_send, g_recv, a_send, a_recv, in_sem,
):
    me = lax.axis_index("tm")
    z = lax.axis_index("heads")
    chips = tm // 2
    span = li_hbm.shape[0]
    heads_here = log_ref.shape[0]
    width = x_ref.shape[1]
    size = width // heads_here
    rows_w = w_hbm.shape[0]
    along = lambda to: (to, z)
    across_z = lambda to: (me, to)
    peer = (lax.rem(me + 1, tm), z)

    loads = [
        pltpu.make_async_copy(src, dst, in_sem.at[k])
        for k, (src, dst) in enumerate((
            (log_hbm, log_ref), (w_hbm, wbuf.at[me]), (x_hbm, x_ref), (dy_hbm, dy_ref),
            (li_hbm, libuf.at[me]),
        ))
    ]
    for made in loads:
        made.start()
    barrier = pltpu.get_barrier_semaphore()
    for d in range(1, tm):
        pl.semaphore_signal(
            barrier, inc=1, device_id=along(lax.rem(me + d, tm)), device_id_type=MESH
        )
    for d in range(1, heads):
        pl.semaphore_signal(
            barrier, inc=1, device_id=across_z(lax.rem(z + d, heads)), device_id_type=MESH
        )

    weights = Gather(wbuf, w_send, w_recv, tm, me, z)
    layer = Gather(libuf, li_send, li_recv, tm, me, z)
    started = []

    row = lax.broadcasted_iota(jnp.int32, (span, span), 0)
    col = lax.broadcasted_iota(jnp.int32, (span, span), 1)
    lower = (row >= col).astype(F32)
    upper = (row <= col).astype(F32)
    strict = (row > col).astype(F32)
    head_of = lax.broadcasted_iota(jnp.int32, (heads_here, width), 0) * size
    place = lax.broadcasted_iota(jnp.int32, (heads_here, width), 1)
    spread = ((place >= head_of) & (place < head_of + size)).astype(F32)
    loads[0].wait()
    sums_t = nn(log_ref[...], upper, HIGH)
    sums = sums_t.T
    wide = nn(sums, spread, HIGH)
    total = wide[span - 1 : span, :]
    dec[me] = jnp.broadcast_to(total, (8, width))
    loads[1].wait()
    pl.semaphore_wait(barrier, tm - 1 + heads - 1)
    weights.start()
    started += exchange(lambda d, to: dec.at[me], dec, d_send, d_recv, tm, me, along)
    loads[2].wait()
    loads[3].wait()
    from_start = jnp.exp(wide)
    to_end = jnp.exp(total - wide)
    x = x_ref[...]
    dy = dy_ref[...]
    x_end = (to_end * x).astype(BF16)
    dy_start = (from_start * dy).astype(BF16)
    x_half = x.astype(BF16)
    dy_half = dy.astype(BF16)

    weights.relay()

    dgx_sum = jnp.zeros((span, span), F32)
    for h in range(heads_here):
        cut = slice(h * size, (h + 1) * size)
        gaps = sums_t[h : h + 1, :] - sums[:, h : h + 1]
        step = jnp.where(row <= col, jnp.exp(jnp.minimum(gaps, 0.0)), 0.0)
        pairs = step * nt(x_half[:, cut], dy_half[:, cut])
        decay[h] = step
        dgx[h] = pairs
        dgx_sum = dgx_sum + pairs

    loads[4].wait()
    sent = []

    def project(chip):
        number = len(sent)
        block = wbuf[pl.ds(2 * chip, 2)].reshape(2 * rows_w, wbuf.shape[2])
        pbuf[chip] = nt(libuf[me], block).astype(BF16)
        part = lax.rem(chip, 2)
        made = []
        for m in range(members):
            to = chip // 2 * members + m
            made.append((to, pltpu.make_async_remote_copy(
                src_ref=pbuf.at[chip],
                dst_ref=bcr.at[z, part],
                send_sem=p_send.at[number, m],
                recv_sem=p_recv.at[z, part],
                device_id=across_z(to),
                device_id_type=MESH,
            )))
        sent.append(made)
        for to, copy in made:
            pl.when(to != z)(copy.start)

    weights.near()
    weights.other(weights.chip)
    project(weights.chip)
    if chips == 4:
        weights.other(weights.xn)
        project(weights.xn)
        weights.other(weights.yn)
        project(weights.yn)
        weights.far()
        layer.first()
        weights.other(weights.dg)
        project(weights.dg)
    else:
        weights.far()
        layer.first()
        for d in range(1, chips):
            chip = lax.rem(weights.chip + d, chips)
            weights.other(chip)
            project(chip)
    group = z // members
    bcr[z] = pbuf[pl.ds(2 * group, 2)]
    for d in range(1, heads):
        other = lax.rem(z + d, heads)
        for part in range(2):
            pltpu.make_async_remote_copy(
                src_ref=bcr.at[other, part],
                dst_ref=bcr.at[other, part],
                send_sem=p_send.at[0, 0],
                recv_sem=p_recv.at[other, part],
                device_id=peer,
                device_id_type=MESH,
            ).wait_recv()
    bc = bcr[0].astype(F32)
    for k in range(1, heads):
        bc = bc + bcr[k].astype(F32)
    b_t = bc[0].T.astype(BF16)
    c_t = bc[1].T.astype(BF16)
    b = bc[0].astype(BF16)
    c = bc[1].astype(BF16)

    st[0] = nn(b_t, x_end).astype(BF16)
    st[1] = nn(c_t, dy_start).astype(BF16)
    chip, core = me // 2, lax.rem(me, 2)

    def state_copy(src, slot, to, number):
        made = pltpu.make_async_remote_copy(
            src_ref=src,
            dst_ref=strecv.at[slot],
            send_sem=s_send.at[number],
            recv_sem=s_recv.at[slot],
            device_id=along(to),
            device_id_type=MESH,
        )
        made.start()
        return made

    for d in range(1, chips):
        to = lax.rem(chip + d, chips) * 2 + core
        started.append(state_copy(st.at[(chip + d) // chips], me, to, d))
    started.append(state_copy(st.at[core], me, chip * 2 + 1 - core, 0))

    cb = nt(b, c)
    after = []
    before = []
    for h in range(heads_here):
        cut = slice(h * size, (h + 1) * size)
        weight = decay[h] * cb
        gx_ref[:, cut] = nn(weight.astype(BF16), dy_half[:, cut])
        product = dgx[h] * cb
        after.append(jnp.sum(product, axis=1, keepdims=True))
        before.append(jnp.sum(product, axis=0, keepdims=True))
    before = jnp.concatenate(before, axis=0)
    after = jnp.concatenate(after, axis=1)
    grad_b = nn(c_t, dgx_sum.T.astype(BF16))
    grad_c = nn(b_t, dgx_sum.astype(BF16))
    inside = nn(strict, after, HIGH) - nt(strict, before, HIGH)

    for d in range(1, chips):
        slot = lax.rem(chip + d, chips) * 2 + core
        landed(strecv, s_send, s_recv, slot, peer).wait_recv()
        started.append(
            state_copy(strecv.at[slot], slot, chip * 2 + 1 - core, chips - 1 + d)
        )
    layer.second()
    layer.relay()
    for d in range(1, tm):
        landed(dec, d_send, d_recv, lax.rem(me + d, tm), peer).wait_recv()
    for d in range(chips):
        slot = lax.rem(chip + d, chips) * 2 + 1 - core
        landed(strecv, s_send, s_recv, slot, peer).wait_recv()
    hin[...] = jnp.zeros_like(hin)
    gout[...] = jnp.zeros_like(gout)

    def forward(q, _):
        hin[...] = hin[...] * jnp.exp(dec[q][0:1, :]) + strecv[q].astype(F32)
        return 0

    def backward(k, _):
        q = tm - 1 - k
        gout[...] = gout[...] * jnp.exp(dec[q][0:1, :]) + strecv[q].astype(F32)
        return 0

    lax.fori_loop(0, me, forward, 0)
    lax.fori_loop(0, tm - 1 - me, backward, 0)
    state = hin[...]
    grad = gout[...]
    state_half = state.astype(BF16)
    grad_half = grad.astype(BF16)
    gbuf[0] = (grad_b + nt(grad_half, x_end)).astype(BF16)
    gbuf[1] = (grad_c + nt(state_half, dy_start)).astype(BF16)
    grecv[z] = gbuf[...]
    started += exchange(lambda d, to: gbuf, grecv, g_send, g_recv, heads, z, across_z)

    from_end = to_end * nn(b, grad_half)
    gx_ref[...] += from_end
    earlier = nt(from_start * nn(c, state_half) * dy, spread, HIGH)
    later = nt(from_end * x, spread, HIGH)
    through = jnp.sum(grad * state, axis=0, keepdims=True) * jnp.exp(total)
    through = nt(jnp.broadcast_to(through, (8, width)), spread, HIGH)
    gl_ref[...] = (
        inside + nn(upper, earlier, HIGH) + nn(strict, later, HIGH) + through[0:1, :]
    ).T

    for d in range(1, heads):
        landed(grecv, g_send, g_recv, lax.rem(z + d, heads), peer).wait_recv()
    turned = []
    for g in range(heads // members):
        for part in range(2):
            acc = grecv[g * members, part].astype(F32)
            for k in range(1, members):
                acc = acc + grecv[g * members + k, part].astype(F32)
            piece = acc.astype(BF16)
            first = (2 * g + part) * N // rows_w
            for k in range(N // rows_w):
                gall[first + k] = piece[k * rows_w : (k + 1) * rows_w]
            turned.append(piece)
    last = exchange(lambda d, to: gall.at[to], grow, a_send, a_recv, tm, me, along)
    grow[me] = gall[me]
    grad_bc = jnp.concatenate([k.astype(F32).T.astype(BF16) for k in turned], axis=1)
    for made in started:
        made.wait_send()
    for made in sent:
        for to, copy in made:
            pl.when(to != z)(copy.wait_send)
    weights.finish()
    layer.near()
    layer.far()
    gi_ref[...] = nn(grad_bc, wbuf[...].reshape(tm * rows_w, wbuf.shape[2])).astype(BF16)

    layer.other(layer.chip)
    for d in range(1, chips):
        layer.other(lax.rem(layer.chip + d, chips))
    for d in range(1, tm):
        landed(grow, a_send, a_recv, lax.rem(me + d, tm), peer).wait_recv()
    rows = jnp.concatenate([grow[k] for k in range(tm)], axis=1)
    gw_ref[...] = nn(rows, libuf[...].reshape(tm * span, libuf.shape[2]))

    for made in last:
        made.wait_send()
    layer.finish()


def store(*refs):
    sems = refs[-1]
    count = (len(refs) - 1) // 2
    copies = [pltpu.make_async_copy(refs[k], refs[count + k], sems.at[k]) for k in range(count)]
    for made in copies:
        made.start()
    for made in copies:
        made.wait()


def solution(mesh):
    tm = mesh.shape["tm"]
    heads = mesh.shape["heads"]
    chips = tm // 2

    def on_device(layer_input, proj_weight, ssd_input, log_decay, out_grad):
        span, depth = layer_input.shape
        rows_w = proj_weight.shape[0]
        heads_here = log_decay.shape[1]
        width = ssd_input.shape[1]
        groups = rows_w * tm // (2 * N)
        members = heads // groups
        copies = 14 if chips == 4 else 4 * (chips - 1) + 2
        dma = lambda *shape: pltpu.SemaphoreType.DMA(shape)
        vmem = pl.BlockSpec(memory_space=pltpu.VMEM)
        hbm = pl.BlockSpec(memory_space=pltpu.HBM)
        shapes = (
            jax.ShapeDtypeStruct((span, width), F32),
            jax.ShapeDtypeStruct((heads_here, span), F32),
            jax.ShapeDtypeStruct((span, depth), BF16),
            jax.ShapeDtypeStruct((rows_w, depth), F32),
        )

        def body(*refs):
            kernel(tm, heads, members, *refs)

        results = pl.pallas_call(
            body,
            out_shape=tuple(pltpu.VMEM(k.shape, k.dtype) for k in shapes),
            in_specs=[hbm] * 5,
            out_specs=(vmem,) * 4,
            scratch_shapes=[
                pltpu.VMEM((span, width), F32),
                pltpu.VMEM((span, width), F32),
                pltpu.VMEM((heads_here, span), F32),
                pltpu.VMEM((tm, rows_w, depth), BF16),
                pltpu.VMEM((tm, span, depth), BF16),
                pltpu.VMEM((tm, 8, width), F32),
                pltpu.VMEM((chips, span, N), BF16),
                pltpu.VMEM((heads, 2, span, N), BF16),
                pltpu.VMEM((2, N, width), BF16),
                pltpu.VMEM((tm, N, width), BF16),
                pltpu.VMEM((N, width), F32),
                pltpu.VMEM((N, width), F32),
                pltpu.VMEM((heads_here, span, span), F32),
                pltpu.VMEM((heads_here, span, span), F32),
                pltpu.VMEM((2, N, span), BF16),
                pltpu.VMEM((heads, 2, N, span), BF16),
                pltpu.VMEM((tm, rows_w, span), BF16),
                pltpu.VMEM((tm, rows_w, span), BF16),
                dma(copies), dma(tm, 2),
                dma(copies), dma(tm, 2),
                dma(tm), dma(tm),
                dma(chips, members), dma(heads, 2),
                dma(tm), dma(tm),
                dma(heads), dma(heads),
                dma(tm), dma(tm),
                dma(5),
            ],
            compiler_params=pltpu.CompilerParams(
                collective_id=0, has_side_effects=True, vmem_limit_bytes=56 * 1024 * 1024
            ),
        )(layer_input, proj_weight, ssd_input, log_decay.T, out_grad)
        grad_x, grad_log, grad_input, grad_weight = pl.pallas_call(
            store,
            out_shape=shapes,
            in_specs=[vmem] * 4,
            out_specs=(hbm,) * 4,
            scratch_shapes=[dma(4)],
            compiler_params=pltpu.CompilerParams(vmem_limit_bytes=1024 * 1024),
        )(*results)
        return grad_x, grad_log.T, grad_input, grad_weight

    return jax.shard_map(
        on_device,
        mesh=mesh,
        in_specs=(P("tm", "heads"),) * 5,
        out_specs=(P("tm", "heads"),) * 4,
        check_vma=False,
    )
```

```python
import jax
import jax.numpy as jnp
from jax import lax
from jax.experimental import pallas as pl
from jax.experimental.pallas import tpu as pltpu
from jax.sharding import PartitionSpec as P

N = 128
MESH = pl.DeviceIdType.MESH
HIGH = lax.Precision.HIGHEST
F32 = jnp.float32
BF16 = jnp.bfloat16


def nn(a, b, precision=None):
    return lax.dot_general(
        a, b, (((1,), (0,)), ((), ())), precision=precision, preferred_element_type=F32
    )


def nt(a, b, precision=None):
    return lax.dot_general(
        a, b, (((1,), (1,)), ((), ())), precision=precision, preferred_element_type=F32
    )


class Gather:
    def __init__(self, buf, send, recv, tm, me, heads_at):
        self.buf, self.send, self.recv = buf, send, recv
        self.tm, self.me, self.z = tm, me, heads_at
        self.chips = tm // 2
        self.chip, self.core = me // 2, lax.rem(me, 2)
        self.half_rows = buf.shape[1] // 2
        self.pending = []
        chip = self.chip
        if self.chips == 4:
            self.xn = chip + 1 - 2 * lax.rem(chip, 2)
            self.yn = lax.rem(chip + 2, 4)
            self.dg = 3 - chip

    def piece(self, slot, half):
        return self.buf.at[slot, pl.ds(half * self.half_rows, self.half_rows)]

    def copy(self, slot, half, chip, core, number):
        part = self.piece(slot, half)
        return pltpu.make_async_remote_copy(
            src_ref=part,
            dst_ref=part,
            send_sem=self.send.at[number],
            recv_sem=self.recv.at[slot, half],
            device_id=(chip * 2 + core, self.z),
            device_id_type=MESH,
        )

    def push(self, slot, half, chip, core):
        made = self.copy(slot, half, chip, core, len(self.pending))
        made.start()
        self.pending.append(made)

    def arrive(self, slot, half):
        self.copy(slot, half, self.chip, 1 - self.core, 0).wait_recv()

    def out(self):
        me, core = self.me, self.core
        if self.chips == 4:
            self.push(me, 0, self.xn, core)
            self.push(me, 1, self.yn, core)
            self.push(me, 1, self.xn, core)
            self.push(me, 0, self.yn, core)
        else:
            for d in range(1, self.chips):
                for half in range(2):
                    self.push(me, half, lax.rem(self.chip + d, self.chips), core)

    def relay(self):
        core = self.core
        if self.chips == 4:
            xs, ys = self.xn * 2 + core, self.yn * 2 + core
            self.arrive(xs, 0)
            self.push(xs, 0, self.yn, core)
            self.arrive(ys, 1)
            self.push(ys, 1, self.xn, core)

    def near(self):
        if self.chips != 4:
            return []
        xs, ys = self.xn * 2 + self.core, self.yn * 2 + self.core
        self.arrive(xs, 1)
        self.arrive(ys, 0)
        return [xs, ys]

    def far(self):
        if self.chips == 4:
            slots = [self.dg * 2 + self.core]
        else:
            slots = [
                lax.rem(self.chip + d, self.chips) * 2 + self.core for d in range(1, self.chips)
            ]
        for slot in slots:
            for half in range(2):
                self.arrive(slot, half)
        return slots

    def share(self, slots):
        for slot in slots:
            for half in range(2):
                self.push(slot, half, self.chip, 1 - self.core)

    def other(self, chip):
        for half in range(2):
            self.arrive(chip * 2 + 1 - self.core, half)

    def finish(self):
        for made in self.pending:
            made.wait_send()


def exchange(src, dst, send, recv, count, me, place):
    copies = []
    for d in range(1, count):
        to = lax.rem(me + d, count)
        copies.append(
            pltpu.make_async_remote_copy(
                src_ref=src(d, to),
                dst_ref=dst.at[me],
                send_sem=send.at[d],
                recv_sem=recv.at[me],
                device_id=place(to),
                device_id_type=MESH,
            )
        )
    for made in copies:
        made.start()
    return copies


def landed(dst, send, recv, slot, to):
    return pltpu.make_async_remote_copy(
        src_ref=dst.at[slot],
        dst_ref=dst.at[slot],
        send_sem=send.at[0],
        recv_sem=recv.at[slot],
        device_id=to,
        device_id_type=MESH,
    )


def kernel(
    tm, heads, members,
    li_hbm, w_hbm, x_hbm, log_hbm, dy_hbm,
    gx_ref, gl_ref, gi_ref, gw_ref,
    x_ref, dy_ref, log_ref,
    wbuf, libuf, dec, pbuf, bcr, st, strecv, hin, gout, decay, dgx, grecv, gall, grow,
    w_send, w_recv, li_send, li_recv, d_send, d_recv, p_send, p_recv, s_send, s_recv,
    g_send, g_recv, a_send, a_recv, in_sem,
):
    me = lax.axis_index("tm")
    z = lax.axis_index("heads")
    chips = tm // 2
    span = li_hbm.shape[0]
    heads_here = log_ref.shape[0]
    width = x_ref.shape[1]
    size = width // heads_here
    rows_w = w_hbm.shape[0]
    along = lambda to: (to, z)
    across_z = lambda to: (me, to)
    peer = (lax.rem(me + 1, tm), z)

    loads = [
        pltpu.make_async_copy(src, dst, in_sem.at[k])
        for k, (src, dst) in enumerate((
            (log_hbm, log_ref), (w_hbm, wbuf.at[me]), (x_hbm, x_ref), (dy_hbm, dy_ref),
            (li_hbm, libuf.at[me]),
        ))
    ]
    for made in loads:
        made.start()
    chip, core = me // 2, lax.rem(me, 2)
    barrier = pltpu.get_barrier_semaphore()
    for d in range(1, tm):
        pl.semaphore_signal(
            barrier, inc=1, device_id=along(lax.rem(me + d, tm)), device_id_type=MESH
        )
    for d in range(1, heads):
        pl.semaphore_signal(
            barrier, inc=1, device_id=across_z(lax.rem(z + d, heads)), device_id_type=MESH
        )
        pl.semaphore_signal(
            barrier,
            inc=1,
            device_id=(chip * 2 + 1 - core, lax.rem(z + d, heads)),
            device_id_type=MESH,
        )

    weights = Gather(wbuf, w_send, w_recv, tm, me, z)
    layer = Gather(libuf, li_send, li_recv, tm, me, z)
    started = []

    row = lax.broadcasted_iota(jnp.int32, (span, span), 0)
    col = lax.broadcasted_iota(jnp.int32, (span, span), 1)
    lower = (row >= col).astype(F32)
    upper = (row <= col).astype(F32)
    strict = (row > col).astype(F32)
    head_of = lax.broadcasted_iota(jnp.int32, (heads_here, width), 0) * size
    place = lax.broadcasted_iota(jnp.int32, (heads_here, width), 1)
    spread = ((place >= head_of) & (place < head_of + size)).astype(F32)
    loads[0].wait()
    sums_t = nn(log_ref[...], upper, HIGH)
    sums = sums_t.T
    wide = nn(sums, spread, HIGH)
    total = wide[span - 1 : span, :]
    dec[me] = jnp.broadcast_to(total, (8, width))
    loads[1].wait()
    pl.semaphore_wait(barrier, tm - 1 + 2 * (heads - 1))
    weights.out()
    loads[4].wait()
    layer.share([me])
    started += exchange(lambda d, to: dec.at[me], dec, d_send, d_recv, tm, me, along)
    loads[2].wait()
    loads[3].wait()
    from_start = jnp.exp(wide)
    to_end = jnp.exp(total - wide)
    x = x_ref[...]
    dy = dy_ref[...]
    x_end = (to_end * x).astype(BF16)
    dy_start = (from_start * dy).astype(BF16)
    x_half = x.astype(BF16)
    dy_half = dy.astype(BF16)

    dgx_sum = jnp.zeros((span, span), F32)

    def pairs_of(h, so_far):
        cut = slice(h * size, (h + 1) * size)
        gaps = sums_t[h : h + 1, :] - sums[:, h : h + 1]
        step = jnp.where(row <= col, jnp.exp(jnp.minimum(gaps, 0.0)), 0.0)
        pairs = step * nt(x_half[:, cut], dy_half[:, cut])
        decay[h] = step
        dgx[h] = pairs
        return so_far + pairs

    for h in range(heads_here // 2):
        dgx_sum = pairs_of(h, dgx_sum)
    weights.relay()

    sent = []

    def project(slot):
        number = len(sent)
        k = slot // 2
        steps = libuf[pl.ds(2 * chip, 2)].reshape(2 * span, libuf.shape[2])
        rows = nt(wbuf[slot], steps).astype(BF16)
        pbuf[k, 0] = rows[:, :span]
        pbuf[k, 1] = rows[:, span:]
        part = lax.rem(k, 2)
        made = []
        for m in range(members):
            to = k // 2 * members + m
            for away in range(2):
                side = core if away == 0 else 1 - core
                made.append((to != z if away == 0 else None, pltpu.make_async_remote_copy(
                    src_ref=pbuf.at[k, side],
                    dst_ref=bcr.at[z, part, core],
                    send_sem=p_send.at[number, 2 * m + away],
                    recv_sem=p_recv.at[z, 2 * part + core],
                    device_id=(chip * 2 + side, to),
                    device_id_type=MESH,
                )))
        sent.append(made)
        for goes, copy in made:
            if goes is None:
                copy.start()
            else:
                pl.when(goes)(copy.start)

    layer.other(chip)
    project(me)
    for h in range(heads_here // 2, heads_here):
        dgx_sum = pairs_of(h, dgx_sum)
    held = weights.near()
    for slot in held:
        project(slot)
    layer.out()
    rest = weights.far()
    for slot in rest:
        project(slot)
    group = z // members
    for part in range(2):
        bcr[z, part, core] = pbuf[2 * group + part, core]

    def bc_landed(source, place):
        pltpu.make_async_remote_copy(
            src_ref=bcr.at[source, place // 2, lax.rem(place, 2)],
            dst_ref=bcr.at[source, place // 2, lax.rem(place, 2)],
            send_sem=p_send.at[0, 0],
            recv_sem=p_recv.at[source, place],
            device_id=peer,
            device_id_type=MESH,
        ).wait_recv()

    for part in range(2):
        bc_landed(z, 2 * part + 1 - core)
    for d in range(1, heads):
        for k in range(4):
            bc_landed(lax.rem(z + d, heads), k)
    bc = bcr[0].astype(F32)
    for k in range(1, heads):
        bc = bc + bcr[k].astype(F32)
    bc = bc.reshape(2, N, span)
    b_t = bc[0].astype(BF16)
    c_t = bc[1].astype(BF16)

    st[0] = nn(b_t, x_end).astype(BF16)
    st[1] = nn(c_t, dy_start).astype(BF16)
    def state_copy(src, slot, to, number):
        made = pltpu.make_async_remote_copy(
            src_ref=src,
            dst_ref=strecv.at[slot],
            send_sem=s_send.at[number],
            recv_sem=s_recv.at[slot],
            device_id=along(to),
            device_id_type=MESH,
        )
        made.start()
        return made

    for d in range(1, chips):
        to = lax.rem(chip + d, chips) * 2 + core
        started.append(state_copy(st.at[(chip + d) // chips], me, to, d))
    started.append(state_copy(st.at[core], me, chip * 2 + 1 - core, 0))

    weights.share([me] + held + rest)
    b = bc[0].T.astype(BF16)
    c = bc[1].T.astype(BF16)

    cb = nt(b, c)
    after = []
    before = []
    for h in range(heads_here):
        cut = slice(h * size, (h + 1) * size)
        weight = decay[h] * cb
        gx_ref[:, cut] = nn(weight.astype(BF16), dy_half[:, cut])
        product = dgx[h] * cb
        after.append(jnp.sum(product, axis=1, keepdims=True))
        before.append(jnp.sum(product, axis=0, keepdims=True))
    before = jnp.concatenate(before, axis=0)
    after = jnp.concatenate(after, axis=1)
    grad_b = nn(c_t, dgx_sum.T.astype(BF16))
    grad_c = nn(b_t, dgx_sum.astype(BF16))
    inside = nn(strict, after, HIGH) - nt(strict, before, HIGH)

    for d in range(1, chips):
        slot = lax.rem(chip + d, chips) * 2 + core
        landed(strecv, s_send, s_recv, slot, peer).wait_recv()
        started.append(
            state_copy(strecv.at[slot], slot, chip * 2 + 1 - core, chips - 1 + d)
        )
    layer.relay()
    for d in range(1, tm):
        landed(dec, d_send, d_recv, lax.rem(me + d, tm), peer).wait_recv()
    for d in range(chips):
        slot = lax.rem(chip + d, chips) * 2 + 1 - core
        landed(strecv, s_send, s_recv, slot, peer).wait_recv()
    hin[...] = jnp.zeros_like(hin)
    gout[...] = jnp.zeros_like(gout)

    def forward(q, _):
        hin[...] = hin[...] * jnp.exp(dec[q][0:1, :]) + strecv[q].astype(F32)
        return 0

    def backward(k, _):
        q = tm - 1 - k
        gout[...] = gout[...] * jnp.exp(dec[q][0:1, :]) + strecv[q].astype(F32)
        return 0

    def send_grad(part, value):
        grecv[z, part] = value.astype(BF16)
        copies = []
        for d in range(1, heads):
            copies.append(pltpu.make_async_remote_copy(
                src_ref=grecv.at[z, part],
                dst_ref=grecv.at[z, part],
                send_sem=g_send.at[d, part],
                recv_sem=g_recv.at[z, part],
                device_id=across_z(lax.rem(z + d, heads)),
                device_id_type=MESH,
            ))
        for made in copies:
            made.start()
        return copies

    lax.fori_loop(0, tm - 1 - me, backward, 0)
    grad = gout[...]
    grad_half = grad.astype(BF16)
    started += send_grad(0, grad_b + nt(grad_half, x_end))
    lax.fori_loop(0, me, forward, 0)
    state = hin[...]
    state_half = state.astype(BF16)
    started += send_grad(1, grad_c + nt(state_half, dy_start))
    layer.share(layer.near())

    from_end = to_end * nn(b, grad_half)
    gx_ref[...] += from_end
    earlier = nt(from_start * nn(c, state_half) * dy, spread, HIGH)
    later = nt(from_end * x, spread, HIGH)
    through = jnp.sum(grad * state, axis=0, keepdims=True) * jnp.exp(total)
    through = nt(jnp.broadcast_to(through, (8, width)), spread, HIGH)
    gl_ref[...] = (
        inside + nn(upper, earlier, HIGH) + nn(strict, later, HIGH) + through[0:1, :]
    ).T

    for d in range(1, heads):
        other = lax.rem(z + d, heads)
        for part in range(2):
            pltpu.make_async_remote_copy(
                src_ref=grecv.at[other, part],
                dst_ref=grecv.at[other, part],
                send_sem=g_send.at[0, 0],
                recv_sem=g_recv.at[other, part],
                device_id=peer,
                device_id_type=MESH,
            ).wait_recv()
    turned = []
    for g in range(heads // members):
        for part in range(2):
            acc = grecv[g * members, part].astype(F32)
            for k in range(1, members):
                acc = acc + grecv[g * members + k, part].astype(F32)
            piece = acc.astype(BF16)
            first = (2 * g + part) * N // rows_w
            for k in range(N // rows_w):
                gall[first + k] = piece[k * rows_w : (k + 1) * rows_w]
            turned.append(piece)
    last = exchange(lambda d, to: gall.at[to], grow, a_send, a_recv, tm, me, along)
    grow[me] = gall[me]
    layer.share(layer.far())
    grad_bc = jnp.concatenate([k.astype(F32).T.astype(BF16) for k in turned], axis=1)
    for made in started:
        made.wait_send()
    for made in sent:
        for goes, copy in made:
            if goes is None:
                copy.wait_send()
            else:
                pl.when(goes)(copy.wait_send)
    for k in range(chips):
        weights.other(k)
    weights.finish()
    gi_ref[...] = nn(grad_bc, wbuf[...].reshape(tm * rows_w, wbuf.shape[2])).astype(BF16)

    for d in range(1, chips):
        layer.other(lax.rem(layer.chip + d, chips))
    for d in range(1, tm):
        landed(grow, a_send, a_recv, lax.rem(me + d, tm), peer).wait_recv()
    rows = jnp.concatenate([grow[k] for k in range(tm)], axis=1)
    gw_ref[...] = nn(rows, libuf[...].reshape(tm * span, libuf.shape[2]))

    for made in last:
        made.wait_send()
    layer.finish()


def store(*refs):
    sems = refs[-1]
    count = (len(refs) - 1) // 2
    copies = [pltpu.make_async_copy(refs[k], refs[count + k], sems.at[k]) for k in range(count)]
    for made in copies:
        made.start()
    for made in copies:
        made.wait()


def solution(mesh):
    tm = mesh.shape["tm"]
    heads = mesh.shape["heads"]
    chips = tm // 2

    def on_device(layer_input, proj_weight, ssd_input, log_decay, out_grad):
        span, depth = layer_input.shape
        rows_w = proj_weight.shape[0]
        heads_here = log_decay.shape[1]
        width = ssd_input.shape[1]
        groups = rows_w * tm // (2 * N)
        members = heads // groups
        copies = 14 if chips == 4 else 4 * (chips - 1) + 2
        dma = lambda *shape: pltpu.SemaphoreType.DMA(shape)
        vmem = pl.BlockSpec(memory_space=pltpu.VMEM)
        hbm = pl.BlockSpec(memory_space=pltpu.HBM)
        shapes = (
            jax.ShapeDtypeStruct((span, width), F32),
            jax.ShapeDtypeStruct((heads_here, span), F32),
            jax.ShapeDtypeStruct((span, depth), BF16),
            jax.ShapeDtypeStruct((rows_w, depth), F32),
        )

        def body(*refs):
            kernel(tm, heads, members, *refs)

        results = pl.pallas_call(
            body,
            out_shape=tuple(pltpu.VMEM(k.shape, k.dtype) for k in shapes),
            in_specs=[hbm] * 5,
            out_specs=(vmem,) * 4,
            scratch_shapes=[
                pltpu.VMEM((span, width), F32),
                pltpu.VMEM((span, width), F32),
                pltpu.VMEM((heads_here, span), F32),
                pltpu.VMEM((tm, rows_w, depth), BF16),
                pltpu.VMEM((tm, span, depth), BF16),
                pltpu.VMEM((tm, 8, width), F32),
                pltpu.VMEM((chips, 2, rows_w, span), BF16),
                pltpu.VMEM((heads, 2, 2, rows_w, span), BF16),
                pltpu.VMEM((2, N, width), BF16),
                pltpu.VMEM((tm, N, width), BF16),
                pltpu.VMEM((N, width), F32),
                pltpu.VMEM((N, width), F32),
                pltpu.VMEM((heads_here, span, span), F32),
                pltpu.VMEM((heads_here, span, span), F32),
                pltpu.VMEM((heads, 2, N, span), BF16),
                pltpu.VMEM((tm, rows_w, span), BF16),
                pltpu.VMEM((tm, rows_w, span), BF16),
                dma(copies), dma(tm, 2),
                dma(copies), dma(tm, 2),
                dma(tm), dma(tm),
                dma(chips, 2 * members), dma(heads, 4),
                dma(tm), dma(tm),
                dma(heads, 2), dma(heads, 2),
                dma(tm), dma(tm),
                dma(5),
            ],
            compiler_params=pltpu.CompilerParams(
                collective_id=0, has_side_effects=True, vmem_limit_bytes=56 * 1024 * 1024
            ),
        )(layer_input, proj_weight, ssd_input, log_decay.T, out_grad)
        grad_x, grad_log, grad_input, grad_weight = pl.pallas_call(
            store,
            out_shape=shapes,
            in_specs=[vmem] * 4,
            out_specs=(hbm,) * 4,
            scratch_shapes=[dma(4)],
            compiler_params=pltpu.CompilerParams(vmem_limit_bytes=1024 * 1024),
        )(*results)
        return grad_x, grad_log.T, grad_input, grad_weight

    return jax.shard_map(
        on_device,
        mesh=mesh,
        in_specs=(P("tm", "heads"),) * 5,
        out_specs=(P("tm", "heads"),) * 4,
        check_vma=False,
    )
```

```python
import jax
import jax.numpy as jnp
from jax import lax
from jax.experimental import pallas as pl
from jax.experimental.pallas import tpu as pltpu
from jax.sharding import PartitionSpec as P

N = 128
MESH = pl.DeviceIdType.MESH
HIGH = lax.Precision.HIGHEST
F32 = jnp.float32
BF16 = jnp.bfloat16


def nn(a, b, precision=None):
    return lax.dot_general(
        a, b, (((1,), (0,)), ((), ())), precision=precision, preferred_element_type=F32
    )


def nt(a, b, precision=None):
    return lax.dot_general(
        a, b, (((1,), (1,)), ((), ())), precision=precision, preferred_element_type=F32
    )


class Gather:
    def __init__(self, buf, send, recv, tm, me, heads_at):
        self.buf, self.send, self.recv = buf, send, recv
        self.tm, self.me, self.z = tm, me, heads_at
        self.chips = tm // 2
        self.chip, self.core = me // 2, lax.rem(me, 2)
        self.half_rows = buf.shape[1] // 2
        self.pending = []
        chip = self.chip
        if self.chips == 4:
            self.xn = chip + 1 - 2 * lax.rem(chip, 2)
            self.yn = lax.rem(chip + 2, 4)
            self.dg = 3 - chip

    def piece(self, slot, half):
        return self.buf.at[slot, pl.ds(half * self.half_rows, self.half_rows)]

    def copy(self, slot, half, chip, core, number):
        part = self.piece(slot, half)
        return pltpu.make_async_remote_copy(
            src_ref=part,
            dst_ref=part,
            send_sem=self.send.at[number],
            recv_sem=self.recv.at[slot, half],
            device_id=(chip * 2 + core, self.z),
            device_id_type=MESH,
        )

    def push(self, slot, half, chip, core):
        made = self.copy(slot, half, chip, core, len(self.pending))
        made.start()
        self.pending.append(made)

    def arrive(self, slot, half):
        self.copy(slot, half, self.chip, 1 - self.core, 0).wait_recv()

    def out(self):
        self.first()
        self.second()

    def first(self):
        me, core = self.me, self.core
        if self.chips == 4:
            self.push(me, 0, self.xn, core)
            self.push(me, 1, self.yn, core)
        else:
            for d in range(1, self.chips):
                self.push(me, 0, lax.rem(self.chip + d, self.chips), core)

    def second(self):
        me, core = self.me, self.core
        if self.chips == 4:
            self.push(me, 1, self.xn, core)
            self.push(me, 0, self.yn, core)
        else:
            for d in range(1, self.chips):
                self.push(me, 1, lax.rem(self.chip + d, self.chips), core)

    def relay(self):
        core = self.core
        if self.chips == 4:
            xs, ys = self.xn * 2 + core, self.yn * 2 + core
            self.arrive(xs, 0)
            self.push(xs, 0, self.yn, core)
            self.arrive(ys, 1)
            self.push(ys, 1, self.xn, core)

    def near(self):
        if self.chips != 4:
            return []
        xs, ys = self.xn * 2 + self.core, self.yn * 2 + self.core
        self.arrive(xs, 1)
        self.arrive(ys, 0)
        return [xs, ys]

    def far(self):
        if self.chips == 4:
            slots = [self.dg * 2 + self.core]
        else:
            slots = [
                lax.rem(self.chip + d, self.chips) * 2 + self.core for d in range(1, self.chips)
            ]
        for slot in slots:
            for half in range(2):
                self.arrive(slot, half)
        return slots

    def share(self, slots):
        for slot in slots:
            for half in range(2):
                self.push(slot, half, self.chip, 1 - self.core)

    def other(self, chip):
        for half in range(2):
            self.arrive(chip * 2 + 1 - self.core, half)

    def finish(self):
        for made in self.pending:
            made.wait_send()


def exchange(src, dst, send, recv, count, me, place):
    copies = []
    for d in range(1, count):
        to = lax.rem(me + d, count)
        copies.append(
            pltpu.make_async_remote_copy(
                src_ref=src(d, to),
                dst_ref=dst.at[me],
                send_sem=send.at[d],
                recv_sem=recv.at[me],
                device_id=place(to),
                device_id_type=MESH,
            )
        )
    for made in copies:
        made.start()
    return copies


def landed(dst, send, recv, slot, to):
    return pltpu.make_async_remote_copy(
        src_ref=dst.at[slot],
        dst_ref=dst.at[slot],
        send_sem=send.at[0],
        recv_sem=recv.at[slot],
        device_id=to,
        device_id_type=MESH,
    )


def kernel(
    tm, heads, members,
    li_hbm, w_hbm, x_hbm, log_hbm, dy_hbm,
    gx_ref, gl_ref, gi_ref, gw_ref,
    x_ref, dy_ref, log_ref,
    wbuf, libuf, dec, pbuf, bcr, st, strecv, hin, gout, decay, dgx, grecv, gall, grow,
    w_send, w_recv, li_send, li_recv, d_send, d_recv, p_send, p_recv, s_send, s_recv,
    g_send, g_recv, a_send, a_recv, in_sem,
):
    me = lax.axis_index("tm")
    z = lax.axis_index("heads")
    chips = tm // 2
    span = li_hbm.shape[0]
    heads_here = log_ref.shape[0]
    width = x_ref.shape[1]
    size = width // heads_here
    rows_w = w_hbm.shape[0]
    along = lambda to: (to, z)
    across_z = lambda to: (me, to)
    peer = (lax.rem(me + 1, tm), z)

    loads = [
        pltpu.make_async_copy(src, dst, in_sem.at[k])
        for k, (src, dst) in enumerate((
            (log_hbm, log_ref), (w_hbm, wbuf.at[me]), (x_hbm, x_ref), (dy_hbm, dy_ref),
            (li_hbm, libuf.at[me]),
        ))
    ]
    for made in loads:
        made.start()
    chip, core = me // 2, lax.rem(me, 2)
    barrier = pltpu.get_barrier_semaphore()
    for d in range(1, tm):
        pl.semaphore_signal(
            barrier, inc=1, device_id=along(lax.rem(me + d, tm)), device_id_type=MESH
        )
    for d in range(1, heads):
        pl.semaphore_signal(
            barrier, inc=1, device_id=across_z(lax.rem(z + d, heads)), device_id_type=MESH
        )
        pl.semaphore_signal(
            barrier,
            inc=1,
            device_id=(chip * 2 + 1 - core, lax.rem(z + d, heads)),
            device_id_type=MESH,
        )

    weights = Gather(wbuf, w_send, w_recv, tm, me, z)
    layer = Gather(libuf, li_send, li_recv, tm, me, z)
    started = []

    row = lax.broadcasted_iota(jnp.int32, (span, span), 0)
    col = lax.broadcasted_iota(jnp.int32, (span, span), 1)
    lower = (row >= col).astype(F32)
    upper = (row <= col).astype(F32)
    strict = (row > col).astype(F32)
    head_of = lax.broadcasted_iota(jnp.int32, (heads_here, width), 0) * size
    place = lax.broadcasted_iota(jnp.int32, (heads_here, width), 1)
    spread = ((place >= head_of) & (place < head_of + size)).astype(F32)
    loads[0].wait()
    sums_t = nn(log_ref[...], upper, HIGH)
    sums = sums_t.T
    wide = nn(sums, spread, HIGH)
    total = wide[span - 1 : span, :]
    dec[me] = jnp.broadcast_to(total, (8, width))
    loads[1].wait()
    pl.semaphore_wait(barrier, tm - 1 + 2 * (heads - 1))
    weights.out()
    loads[4].wait()
    layer.share([me])
    started += exchange(lambda d, to: dec.at[me], dec, d_send, d_recv, tm, me, along)
    loads[2].wait()
    loads[3].wait()
    from_start = jnp.exp(wide)
    to_end = jnp.exp(total - wide)
    x = x_ref[...]
    dy = dy_ref[...]
    x_end = (to_end * x).astype(BF16)
    dy_start = (from_start * dy).astype(BF16)
    x_half = x.astype(BF16)
    dy_half = dy.astype(BF16)

    dgx_sum = jnp.zeros((span, span), F32)

    def pairs_of(h, so_far):
        cut = slice(h * size, (h + 1) * size)
        gaps = sums_t[h : h + 1, :] - sums[:, h : h + 1]
        step = jnp.where(row <= col, jnp.exp(jnp.minimum(gaps, 0.0)), 0.0)
        pairs = step * nt(x_half[:, cut], dy_half[:, cut])
        decay[h] = step
        dgx[h] = pairs
        return so_far + pairs

    for h in range(heads_here // 2):
        dgx_sum = pairs_of(h, dgx_sum)
    weights.relay()

    sent = []

    def project(slot):
        number = len(sent)
        k = slot // 2
        steps = libuf[pl.ds(2 * chip, 2)].reshape(2 * span, libuf.shape[2])
        rows = nt(wbuf[slot], steps).astype(BF16)
        pbuf[k, 0] = rows[:, :span]
        pbuf[k, 1] = rows[:, span:]
        part = lax.rem(k, 2)
        made = []
        for m in range(members):
            to = k // 2 * members + m
            for away in range(2):
                side = core if away == 0 else 1 - core
                made.append((to != z if away == 0 else None, pltpu.make_async_remote_copy(
                    src_ref=pbuf.at[k, side],
                    dst_ref=bcr.at[z, part, core],
                    send_sem=p_send.at[number, 2 * m + away],
                    recv_sem=p_recv.at[z, 2 * part + core],
                    device_id=(chip * 2 + side, to),
                    device_id_type=MESH,
                )))
        sent.append(made)
        for goes, copy in made:
            if goes is None:
                copy.start()
            else:
                pl.when(goes)(copy.start)

    layer.other(chip)
    project(me)
    for h in range(heads_here // 2, heads_here):
        dgx_sum = pairs_of(h, dgx_sum)
    held = weights.near()
    for slot in held:
        project(slot)
    rest = weights.far()
    for slot in rest:
        project(slot)
    layer.first()
    group = z // members
    for part in range(2):
        bcr[z, part, core] = pbuf[2 * group + part, core]

    def bc_landed(source, place):
        pltpu.make_async_remote_copy(
            src_ref=bcr.at[source, place // 2, lax.rem(place, 2)],
            dst_ref=bcr.at[source, place // 2, lax.rem(place, 2)],
            send_sem=p_send.at[0, 0],
            recv_sem=p_recv.at[source, place],
            device_id=peer,
            device_id_type=MESH,
        ).wait_recv()

    for part in range(2):
        bc_landed(z, 2 * part + 1 - core)
    for d in range(1, heads):
        for k in range(4):
            bc_landed(lax.rem(z + d, heads), k)
    bc = bcr[0].astype(F32)
    for k in range(1, heads):
        bc = bc + bcr[k].astype(F32)
    bc = bc.reshape(2, N, span)
    b_t = bc[0].astype(BF16)
    c_t = bc[1].astype(BF16)

    st[0] = nn(b_t, x_end).astype(BF16)
    st[1] = nn(c_t, dy_start).astype(BF16)
    def state_copy(src, slot, to, number):
        made = pltpu.make_async_remote_copy(
            src_ref=src,
            dst_ref=strecv.at[slot],
            send_sem=s_send.at[number],
            recv_sem=s_recv.at[slot],
            device_id=along(to),
            device_id_type=MESH,
        )
        made.start()
        return made

    for d in range(1, chips):
        to = lax.rem(chip + d, chips) * 2 + core
        started.append(state_copy(st.at[(chip + d) // chips], me, to, d))
    started.append(state_copy(st.at[core], me, chip * 2 + 1 - core, 0))

    weights.share([me] + held + rest)
    b = bc[0].T.astype(BF16)
    c = bc[1].T.astype(BF16)

    cb = nt(b, c)
    after = []
    before = []
    for h in range(heads_here):
        cut = slice(h * size, (h + 1) * size)
        weight = decay[h] * cb
        gx_ref[:, cut] = nn(weight.astype(BF16), dy_half[:, cut])
        product = dgx[h] * cb
        after.append(jnp.sum(product, axis=1, keepdims=True))
        before.append(jnp.sum(product, axis=0, keepdims=True))
    before = jnp.concatenate(before, axis=0)
    after = jnp.concatenate(after, axis=1)
    grad_b = nn(c_t, dgx_sum.T.astype(BF16))
    grad_c = nn(b_t, dgx_sum.astype(BF16))
    inside = nn(strict, after, HIGH) - nt(strict, before, HIGH)

    for d in range(1, chips):
        slot = lax.rem(chip + d, chips) * 2 + core
        landed(strecv, s_send, s_recv, slot, peer).wait_recv()
        started.append(
            state_copy(strecv.at[slot], slot, chip * 2 + 1 - core, chips - 1 + d)
        )
    layer.second()
    layer.relay()
    for d in range(1, tm):
        landed(dec, d_send, d_recv, lax.rem(me + d, tm), peer).wait_recv()
    for d in range(chips):
        slot = lax.rem(chip + d, chips) * 2 + 1 - core
        landed(strecv, s_send, s_recv, slot, peer).wait_recv()
    hin[...] = jnp.zeros_like(hin)
    gout[...] = jnp.zeros_like(gout)

    def forward(q, _):
        hin[...] = hin[...] * jnp.exp(dec[q][0:1, :]) + strecv[q].astype(F32)
        return 0

    def backward(k, _):
        q = tm - 1 - k
        gout[...] = gout[...] * jnp.exp(dec[q][0:1, :]) + strecv[q].astype(F32)
        return 0

    def send_grad(part, value):
        grecv[z, part] = value.astype(BF16)
        copies = []
        for d in range(1, heads):
            copies.append(pltpu.make_async_remote_copy(
                src_ref=grecv.at[z, part],
                dst_ref=grecv.at[z, part],
                send_sem=g_send.at[d, part],
                recv_sem=g_recv.at[z, part],
                device_id=across_z(lax.rem(z + d, heads)),
                device_id_type=MESH,
            ))
        for made in copies:
            made.start()
        return copies

    lax.fori_loop(0, tm - 1 - me, backward, 0)
    grad = gout[...]
    grad_half = grad.astype(BF16)
    started += send_grad(0, grad_b + nt(grad_half, x_end))
    lax.fori_loop(0, me, forward, 0)
    state = hin[...]
    state_half = state.astype(BF16)
    started += send_grad(1, grad_c + nt(state_half, dy_start))

    from_end = to_end * nn(b, grad_half)
    gx_ref[...] += from_end
    earlier = nt(from_start * nn(c, state_half) * dy, spread, HIGH)
    later = nt(from_end * x, spread, HIGH)
    through = jnp.sum(grad * state, axis=0, keepdims=True) * jnp.exp(total)
    through = nt(jnp.broadcast_to(through, (8, width)), spread, HIGH)
    gl_ref[...] = (
        inside + nn(upper, earlier, HIGH) + nn(strict, later, HIGH) + through[0:1, :]
    ).T

    for d in range(1, heads):
        other = lax.rem(z + d, heads)
        for part in range(2):
            pltpu.make_async_remote_copy(
                src_ref=grecv.at[other, part],
                dst_ref=grecv.at[other, part],
                send_sem=g_send.at[0, 0],
                recv_sem=g_recv.at[other, part],
                device_id=peer,
                device_id_type=MESH,
            ).wait_recv()
    turned = []
    for g in range(heads // members):
        for part in range(2):
            acc = grecv[g * members, part].astype(F32)
            for k in range(1, members):
                acc = acc + grecv[g * members + k, part].astype(F32)
            piece = acc.astype(BF16)
            first = (2 * g + part) * N // rows_w
            for k in range(N // rows_w):
                gall[first + k] = piece[k * rows_w : (k + 1) * rows_w]
            turned.append(piece)
    last = exchange(lambda d, to: gall.at[to], grow, a_send, a_recv, tm, me, along)
    grow[me] = gall[me]
    layer.share(layer.near())
    layer.share(layer.far())
    grad_bc = jnp.concatenate([k.astype(F32).T.astype(BF16) for k in turned], axis=1)
    for made in started:
        made.wait_send()
    for made in sent:
        for goes, copy in made:
            if goes is None:
                copy.wait_send()
            else:
                pl.when(goes)(copy.wait_send)
    for k in range(chips):
        weights.other(k)
    weights.finish()
    gi_ref[...] = nn(grad_bc, wbuf[...].reshape(tm * rows_w, wbuf.shape[2])).astype(BF16)

    for d in range(1, chips):
        layer.other(lax.rem(layer.chip + d, chips))
    for d in range(1, tm):
        landed(grow, a_send, a_recv, lax.rem(me + d, tm), peer).wait_recv()
    rows = jnp.concatenate([grow[k] for k in range(tm)], axis=1)
    gw_ref[...] = nn(rows, libuf[...].reshape(tm * span, libuf.shape[2]))

    for made in last:
        made.wait_send()
    layer.finish()


def store(*refs):
    sems = refs[-1]
    count = (len(refs) - 1) // 2
    copies = [pltpu.make_async_copy(refs[k], refs[count + k], sems.at[k]) for k in range(count)]
    for made in copies:
        made.start()
    for made in copies:
        made.wait()


def solution(mesh):
    tm = mesh.shape["tm"]
    heads = mesh.shape["heads"]
    chips = tm // 2

    def on_device(layer_input, proj_weight, ssd_input, log_decay, out_grad):
        span, depth = layer_input.shape
        rows_w = proj_weight.shape[0]
        heads_here = log_decay.shape[1]
        width = ssd_input.shape[1]
        groups = rows_w * tm // (2 * N)
        members = heads // groups
        copies = 14 if chips == 4 else 4 * (chips - 1) + 2
        dma = lambda *shape: pltpu.SemaphoreType.DMA(shape)
        vmem = pl.BlockSpec(memory_space=pltpu.VMEM)
        hbm = pl.BlockSpec(memory_space=pltpu.HBM)
        shapes = (
            jax.ShapeDtypeStruct((span, width), F32),
            jax.ShapeDtypeStruct((heads_here, span), F32),
            jax.ShapeDtypeStruct((span, depth), BF16),
            jax.ShapeDtypeStruct((rows_w, depth), F32),
        )

        def body(*refs):
            kernel(tm, heads, members, *refs)

        results = pl.pallas_call(
            body,
            out_shape=tuple(pltpu.VMEM(k.shape, k.dtype) for k in shapes),
            in_specs=[hbm] * 5,
            out_specs=(vmem,) * 4,
            scratch_shapes=[
                pltpu.VMEM((span, width), F32),
                pltpu.VMEM((span, width), F32),
                pltpu.VMEM((heads_here, span), F32),
                pltpu.VMEM((tm, rows_w, depth), BF16),
                pltpu.VMEM((tm, span, depth), BF16),
                pltpu.VMEM((tm, 8, width), F32),
                pltpu.VMEM((chips, 2, rows_w, span), BF16),
                pltpu.VMEM((heads, 2, 2, rows_w, span), BF16),
                pltpu.VMEM((2, N, width), BF16),
                pltpu.VMEM((tm, N, width), BF16),
                pltpu.VMEM((N, width), F32),
                pltpu.VMEM((N, width), F32),
                pltpu.VMEM((heads_here, span, span), F32),
                pltpu.VMEM((heads_here, span, span), F32),
                pltpu.VMEM((heads, 2, N, span), BF16),
                pltpu.VMEM((tm, rows_w, span), BF16),
                pltpu.VMEM((tm, rows_w, span), BF16),
                dma(copies), dma(tm, 2),
                dma(copies), dma(tm, 2),
                dma(tm), dma(tm),
                dma(chips, 2 * members), dma(heads, 4),
                dma(tm), dma(tm),
                dma(heads, 2), dma(heads, 2),
                dma(tm), dma(tm),
                dma(5),
            ],
            compiler_params=pltpu.CompilerParams(
                collective_id=0, has_side_effects=True, vmem_limit_bytes=56 * 1024 * 1024
            ),
        )(layer_input, proj_weight, ssd_input, log_decay.T, out_grad)
        grad_x, grad_log, grad_input, grad_weight = pl.pallas_call(
            store,
            out_shape=shapes,
            in_specs=[vmem] * 4,
            out_specs=(hbm,) * 4,
            scratch_shapes=[dma(4)],
            compiler_params=pltpu.CompilerParams(vmem_limit_bytes=1024 * 1024),
        )(*results)
        return grad_x, grad_log.T, grad_input, grad_weight

    return jax.shard_map(
        on_device,
        mesh=mesh,
        in_specs=(P("tm", "heads"),) * 5,
        out_specs=(P("tm", "heads"),) * 4,
        check_vma=False,
    )
```

```python
import jax
import jax.numpy as jnp
from jax import lax
from jax.experimental import pallas as pl
from jax.experimental.pallas import tpu as pltpu
from jax.sharding import PartitionSpec as P

N = 128
MESH = pl.DeviceIdType.MESH
HIGH = lax.Precision.HIGHEST
F32 = jnp.float32
BF16 = jnp.bfloat16


def nn(a, b, precision=None):
    return lax.dot_general(
        a, b, (((1,), (0,)), ((), ())), precision=precision, preferred_element_type=F32
    )


def nt(a, b, precision=None):
    return lax.dot_general(
        a, b, (((1,), (1,)), ((), ())), precision=precision, preferred_element_type=F32
    )


class Gather:
    def __init__(self, buf, send, recv, tm, me, heads_at):
        self.buf, self.send, self.recv = buf, send, recv
        self.tm, self.me, self.z = tm, me, heads_at
        self.chips = tm // 2
        self.chip, self.core = me // 2, lax.rem(me, 2)
        self.half_rows = buf.shape[1] // 2
        self.pending = []
        chip = self.chip
        if self.chips == 4:
            self.xn = chip + 1 - 2 * lax.rem(chip, 2)
            self.yn = lax.rem(chip + 2, 4)
            self.dg = 3 - chip

    def piece(self, slot, half):
        return self.buf.at[slot, pl.ds(half * self.half_rows, self.half_rows)]

    def copy(self, slot, half, chip, core, number):
        part = self.piece(slot, half)
        return pltpu.make_async_remote_copy(
            src_ref=part,
            dst_ref=part,
            send_sem=self.send.at[number],
            recv_sem=self.recv.at[slot, half],
            device_id=(chip * 2 + core, self.z),
            device_id_type=MESH,
        )

    def push(self, slot, half, chip, core):
        made = self.copy(slot, half, chip, core, len(self.pending))
        made.start()
        self.pending.append(made)

    def arrive(self, slot, half):
        self.copy(slot, half, self.chip, 1 - self.core, 0).wait_recv()

    def out(self):
        self.first()
        self.second()

    def first(self):
        me, core = self.me, self.core
        if self.chips == 4:
            self.push(me, 0, self.xn, core)
            self.push(me, 1, self.yn, core)
        else:
            for d in range(1, self.chips):
                self.push(me, 0, lax.rem(self.chip + d, self.chips), core)

    def second(self):
        me, core = self.me, self.core
        if self.chips == 4:
            self.push(me, 1, self.xn, core)
            self.push(me, 0, self.yn, core)
        else:
            for d in range(1, self.chips):
                self.push(me, 1, lax.rem(self.chip + d, self.chips), core)

    def relay(self):
        core = self.core
        if self.chips == 4:
            xs, ys = self.xn * 2 + core, self.yn * 2 + core
            self.arrive(xs, 0)
            self.push(xs, 0, self.yn, core)
            self.arrive(ys, 1)
            self.push(ys, 1, self.xn, core)

    def near(self):
        if self.chips != 4:
            return []
        xs, ys = self.xn * 2 + self.core, self.yn * 2 + self.core
        self.arrive(xs, 1)
        self.arrive(ys, 0)
        return [xs, ys]

    def far(self):
        if self.chips == 4:
            slots = [self.dg * 2 + self.core]
        else:
            slots = [
                lax.rem(self.chip + d, self.chips) * 2 + self.core for d in range(1, self.chips)
            ]
        for slot in slots:
            for half in range(2):
                self.arrive(slot, half)
        return slots

    def share(self, slots):
        for slot in slots:
            for half in range(2):
                self.push(slot, half, self.chip, 1 - self.core)

    def other(self, chip):
        for half in range(2):
            self.arrive(chip * 2 + 1 - self.core, half)

    def finish(self):
        for made in self.pending:
            made.wait_send()


def exchange(src, dst, send, recv, count, me, place):
    copies = []
    for d in range(1, count):
        to = lax.rem(me + d, count)
        copies.append(
            pltpu.make_async_remote_copy(
                src_ref=src(d, to),
                dst_ref=dst.at[me],
                send_sem=send.at[d],
                recv_sem=recv.at[me],
                device_id=place(to),
                device_id_type=MESH,
            )
        )
    for made in copies:
        made.start()
    return copies


def landed(dst, send, recv, slot, to):
    return pltpu.make_async_remote_copy(
        src_ref=dst.at[slot],
        dst_ref=dst.at[slot],
        send_sem=send.at[0],
        recv_sem=recv.at[slot],
        device_id=to,
        device_id_type=MESH,
    )


def kernel(
    tm, heads, members,
    li_hbm, w_hbm, x_hbm, log_hbm, dy_hbm,
    gx_ref, gl_ref, gi_ref, gw_ref,
    x_ref, dy_ref, log_ref,
    wbuf, libuf, dec, pbuf, bcr, st, strecv, hin, gout, decay, dgx, lit, grecv, gall, grow,
    w_send, w_recv, li_send, li_recv, d_send, d_recv, p_send, p_recv, s_send, s_recv,
    g_send, g_recv, a_send, a_recv, in_sem,
):
    me = lax.axis_index("tm")
    z = lax.axis_index("heads")
    chips = tm // 2
    span = li_hbm.shape[0]
    heads_here = log_ref.shape[0]
    width = x_ref.shape[1]
    size = width // heads_here
    rows_w = w_hbm.shape[0]
    along = lambda to: (to, z)
    across_z = lambda to: (me, to)
    peer = (lax.rem(me + 1, tm), z)

    loads = [
        pltpu.make_async_copy(src, dst, in_sem.at[k])
        for k, (src, dst) in enumerate((
            (log_hbm, log_ref), (w_hbm, wbuf.at[me]), (x_hbm, x_ref), (dy_hbm, dy_ref),
            (li_hbm, libuf.at[me]),
        ))
    ]
    for made in loads:
        made.start()
    chip, core = me // 2, lax.rem(me, 2)
    barrier = pltpu.get_barrier_semaphore()
    for d in range(1, tm):
        pl.semaphore_signal(
            barrier, inc=1, device_id=along(lax.rem(me + d, tm)), device_id_type=MESH
        )
    for d in range(1, heads):
        pl.semaphore_signal(
            barrier, inc=1, device_id=across_z(lax.rem(z + d, heads)), device_id_type=MESH
        )
        pl.semaphore_signal(
            barrier,
            inc=1,
            device_id=(chip * 2 + 1 - core, lax.rem(z + d, heads)),
            device_id_type=MESH,
        )

    weights = Gather(wbuf, w_send, w_recv, tm, me, z)
    layer = Gather(libuf, li_send, li_recv, tm, me, z)
    started = []

    row = lax.broadcasted_iota(jnp.int32, (span, span), 0)
    col = lax.broadcasted_iota(jnp.int32, (span, span), 1)
    lower = (row >= col).astype(F32)
    upper = (row <= col).astype(F32)
    strict = (row > col).astype(F32)
    head_of = lax.broadcasted_iota(jnp.int32, (heads_here, width), 0) * size
    place = lax.broadcasted_iota(jnp.int32, (heads_here, width), 1)
    spread = ((place >= head_of) & (place < head_of + size)).astype(F32)
    loads[0].wait()
    sums_t = nn(log_ref[...], upper, HIGH)
    sums = sums_t.T
    wide = nn(sums, spread, HIGH)
    total = wide[span - 1 : span, :]
    dec[me] = jnp.broadcast_to(total, (8, width))
    loads[1].wait()
    pl.semaphore_wait(barrier, tm - 1 + 2 * (heads - 1))
    weights.out()
    loads[4].wait()
    layer.share([me])
    started += exchange(lambda d, to: dec.at[me], dec, d_send, d_recv, tm, me, along)
    loads[2].wait()
    loads[3].wait()
    from_start = jnp.exp(wide)
    to_end = jnp.exp(total - wide)
    x = x_ref[...]
    dy = dy_ref[...]
    x_end = to_end * x
    dy_start = from_start * dy
    x_end_t = x_end.T.astype(BF16)
    dy_start_t = dy_start.T.astype(BF16)
    x_end = x_end.astype(BF16)
    dy_start = dy_start.astype(BF16)
    lit[:, :span] = libuf[me].T
    x_half = x.astype(BF16)
    dy_half = dy.astype(BF16)

    dgx_sum = jnp.zeros((span, span), F32)

    def pairs_of(h, so_far):
        cut = slice(h * size, (h + 1) * size)
        gaps = sums_t[h : h + 1, :] - sums[:, h : h + 1]
        step = jnp.where(row <= col, jnp.exp(jnp.minimum(gaps, 0.0)), 0.0)
        pairs = step * nt(x_half[:, cut], dy_half[:, cut])
        decay[h] = step
        dgx[h] = pairs
        return so_far + pairs

    weights.relay()

    sent = []

    def project(slot):
        number = len(sent)
        k = slot // 2
        rows = nn(wbuf[slot], lit[...]).astype(BF16)
        pbuf[k, 0] = rows[:, :span]
        pbuf[k, 1] = rows[:, span:]
        part = lax.rem(k, 2)
        made = []
        for m in range(members):
            to = k // 2 * members + m
            for away in range(2):
                side = core if away == 0 else 1 - core
                made.append((to != z if away == 0 else None, pltpu.make_async_remote_copy(
                    src_ref=pbuf.at[k, away],
                    dst_ref=bcr.at[z, part, core],
                    send_sem=p_send.at[number, 2 * m + away],
                    recv_sem=p_recv.at[z, 2 * part + core],
                    device_id=(chip * 2 + side, to),
                    device_id_type=MESH,
                )))
        sent.append(made)
        for goes, copy in made:
            if goes is None:
                copy.start()
            else:
                pl.when(goes)(copy.start)

    layer.other(chip)
    lit[:, span:] = libuf[chip * 2 + 1 - core].T
    project(me)
    for h in range(heads_here):
        dgx_sum = pairs_of(h, dgx_sum)
    held = weights.near()
    for slot in held:
        project(slot)
    rest = weights.far()
    for slot in rest:
        project(slot)
    layer.first()
    group = z // members
    for part in range(2):
        bcr[z, part, core] = pbuf[2 * group + part, 0]

    def bc_landed(source, place):
        pltpu.make_async_remote_copy(
            src_ref=bcr.at[source, place // 2, lax.rem(place, 2)],
            dst_ref=bcr.at[source, place // 2, lax.rem(place, 2)],
            send_sem=p_send.at[0, 0],
            recv_sem=p_recv.at[source, place],
            device_id=peer,
            device_id_type=MESH,
        ).wait_recv()

    for part in range(2):
        bc_landed(z, 2 * part + 1 - core)
    for d in range(1, heads):
        for k in range(4):
            bc_landed(lax.rem(z + d, heads), k)
    bc = bcr[0].astype(F32)
    for k in range(1, heads):
        bc = bc + bcr[k].astype(F32)
    bc = bc.reshape(2, N, span)
    b_t = bc[0].astype(BF16)
    c_t = bc[1].astype(BF16)

    st[0] = nn(b_t, x_end).astype(BF16)
    st[1] = nn(c_t, dy_start).astype(BF16)
    def state_copy(src, slot, to, number):
        made = pltpu.make_async_remote_copy(
            src_ref=src,
            dst_ref=strecv.at[slot],
            send_sem=s_send.at[number],
            recv_sem=s_recv.at[slot],
            device_id=along(to),
            device_id_type=MESH,
        )
        made.start()
        return made

    for d in range(1, chips):
        to = lax.rem(chip + d, chips) * 2 + core
        started.append(state_copy(st.at[(chip + d) // chips], me, to, d))
    started.append(state_copy(st.at[core], me, chip * 2 + 1 - core, 0))

    weights.share([me] + held + rest)
    b = bc[0].T.astype(BF16)
    c = bc[1].T.astype(BF16)

    cb = nn(b, c_t)
    after = []
    before = []
    for h in range(heads_here):
        cut = slice(h * size, (h + 1) * size)
        weight = decay[h] * cb
        gx_ref[:, cut] = nn(weight.astype(BF16), dy_half[:, cut])
        product = dgx[h] * cb
        after.append(jnp.sum(product, axis=1, keepdims=True))
        before.append(jnp.sum(product, axis=0, keepdims=True))
    before = jnp.concatenate(before, axis=0)
    after = jnp.concatenate(after, axis=1)
    grad_b = nn(c_t, dgx_sum.T.astype(BF16))
    grad_c = nn(b_t, dgx_sum.astype(BF16))
    inside = nn(strict, after, HIGH) - nt(strict, before, HIGH)

    for d in range(1, chips):
        slot = lax.rem(chip + d, chips) * 2 + core
        landed(strecv, s_send, s_recv, slot, peer).wait_recv()
        started.append(
            state_copy(strecv.at[slot], slot, chip * 2 + 1 - core, chips - 1 + d)
        )
    layer.second()
    layer.relay()
    for d in range(1, tm):
        landed(dec, d_send, d_recv, lax.rem(me + d, tm), peer).wait_recv()
    for d in range(chips):
        slot = lax.rem(chip + d, chips) * 2 + 1 - core
        landed(strecv, s_send, s_recv, slot, peer).wait_recv()
    hin[...] = jnp.zeros_like(hin)
    gout[...] = jnp.zeros_like(gout)

    def forward(q, _):
        hin[...] = hin[...] * jnp.exp(dec[q][0:1, :]) + strecv[q].astype(F32)
        return 0

    def backward(k, _):
        q = tm - 1 - k
        gout[...] = gout[...] * jnp.exp(dec[q][0:1, :]) + strecv[q].astype(F32)
        return 0

    def send_grad(part, value):
        grecv[z, part] = value.astype(BF16)
        copies = []
        for d in range(1, heads):
            copies.append(pltpu.make_async_remote_copy(
                src_ref=grecv.at[z, part],
                dst_ref=grecv.at[z, part],
                send_sem=g_send.at[d, part],
                recv_sem=g_recv.at[z, part],
                device_id=across_z(lax.rem(z + d, heads)),
                device_id_type=MESH,
            ))
        for made in copies:
            made.start()
        return copies

    lax.fori_loop(0, tm - 1 - me, backward, 0)
    grad = gout[...]
    grad_half = grad.astype(BF16)
    started += send_grad(0, grad_b + nn(grad_half, x_end_t))
    lax.fori_loop(0, me, forward, 0)
    state = hin[...]
    state_half = state.astype(BF16)
    started += send_grad(1, grad_c + nn(state_half, dy_start_t))

    from_end = to_end * nn(b, grad_half)
    gx_ref[...] += from_end
    earlier = nt(from_start * nn(c, state_half) * dy, spread, HIGH)
    later = nt(from_end * x, spread, HIGH)
    through = jnp.sum(grad * state, axis=0, keepdims=True) * jnp.exp(total)
    through = nt(jnp.broadcast_to(through, (8, width)), spread, HIGH)
    gl_ref[...] = (
        inside + nn(upper, earlier, HIGH) + nn(strict, later, HIGH) + through[0:1, :]
    ).T

    for d in range(1, heads):
        other = lax.rem(z + d, heads)
        for part in range(2):
            pltpu.make_async_remote_copy(
                src_ref=grecv.at[other, part],
                dst_ref=grecv.at[other, part],
                send_sem=g_send.at[0, 0],
                recv_sem=g_recv.at[other, part],
                device_id=peer,
                device_id_type=MESH,
            ).wait_recv()
    turned = []
    for g in range(heads // members):
        for part in range(2):
            acc = grecv[g * members, part].astype(F32)
            for k in range(1, members):
                acc = acc + grecv[g * members + k, part].astype(F32)
            piece = acc.astype(BF16)
            first = (2 * g + part) * N // rows_w
            for k in range(N // rows_w):
                gall[first + k] = piece[k * rows_w : (k + 1) * rows_w]
            turned.append(piece)
    last = exchange(lambda d, to: gall.at[to], grow, a_send, a_recv, tm, me, along)
    grow[me] = gall[me]
    layer.share(layer.near())
    layer.share(layer.far())
    grad_bc = jnp.concatenate([k.astype(F32).T.astype(BF16) for k in turned], axis=1)
    for made in started:
        made.wait_send()
    for made in sent:
        for goes, copy in made:
            if goes is None:
                copy.wait_send()
            else:
                pl.when(goes)(copy.wait_send)
    for k in range(chips):
        weights.other(k)
    weights.finish()
    gi_ref[...] = nn(grad_bc, wbuf[...].reshape(tm * rows_w, wbuf.shape[2])).astype(BF16)

    for d in range(1, chips):
        layer.other(lax.rem(layer.chip + d, chips))
    for d in range(1, tm):
        landed(grow, a_send, a_recv, lax.rem(me + d, tm), peer).wait_recv()
    rows = jnp.concatenate([grow[k] for k in range(tm)], axis=1)
    gw_ref[...] = nn(rows, libuf[...].reshape(tm * span, libuf.shape[2]))

    for made in last:
        made.wait_send()
    layer.finish()


def store(*refs):
    sems = refs[-1]
    count = (len(refs) - 1) // 2
    copies = [pltpu.make_async_copy(refs[k], refs[count + k], sems.at[k]) for k in range(count)]
    for made in copies:
        made.start()
    for made in copies:
        made.wait()


def solution(mesh):
    tm = mesh.shape["tm"]
    heads = mesh.shape["heads"]
    chips = tm // 2

    def on_device(layer_input, proj_weight, ssd_input, log_decay, out_grad):
        span, depth = layer_input.shape
        rows_w = proj_weight.shape[0]
        heads_here = log_decay.shape[1]
        width = ssd_input.shape[1]
        groups = rows_w * tm // (2 * N)
        members = heads // groups
        copies = 14 if chips == 4 else 4 * (chips - 1) + 2
        dma = lambda *shape: pltpu.SemaphoreType.DMA(shape)
        vmem = pl.BlockSpec(memory_space=pltpu.VMEM)
        hbm = pl.BlockSpec(memory_space=pltpu.HBM)
        shapes = (
            jax.ShapeDtypeStruct((span, width), F32),
            jax.ShapeDtypeStruct((heads_here, span), F32),
            jax.ShapeDtypeStruct((span, depth), BF16),
            jax.ShapeDtypeStruct((rows_w, depth), F32),
        )

        def body(*refs):
            kernel(tm, heads, members, *refs)

        results = pl.pallas_call(
            body,
            out_shape=tuple(pltpu.VMEM(k.shape, k.dtype) for k in shapes),
            in_specs=[hbm] * 5,
            out_specs=(vmem,) * 4,
            scratch_shapes=[
                pltpu.VMEM((span, width), F32),
                pltpu.VMEM((span, width), F32),
                pltpu.VMEM((heads_here, span), F32),
                pltpu.VMEM((tm, rows_w, depth), BF16),
                pltpu.VMEM((tm, span, depth), BF16),
                pltpu.VMEM((tm, 8, width), F32),
                pltpu.VMEM((chips, 2, rows_w, span), BF16),
                pltpu.VMEM((heads, 2, 2, rows_w, span), BF16),
                pltpu.VMEM((2, N, width), BF16),
                pltpu.VMEM((tm, N, width), BF16),
                pltpu.VMEM((N, width), F32),
                pltpu.VMEM((N, width), F32),
                pltpu.VMEM((heads_here, span, span), F32),
                pltpu.VMEM((heads_here, span, span), F32),
                pltpu.VMEM((depth, 2 * span), BF16),
                pltpu.VMEM((heads, 2, N, span), BF16),
                pltpu.VMEM((tm, rows_w, span), BF16),
                pltpu.VMEM((tm, rows_w, span), BF16),
                dma(copies), dma(tm, 2),
                dma(copies), dma(tm, 2),
                dma(tm), dma(tm),
                dma(chips, 2 * members), dma(heads, 4),
                dma(tm), dma(tm),
                dma(heads, 2), dma(heads, 2),
                dma(tm), dma(tm),
                dma(5),
            ],
            compiler_params=pltpu.CompilerParams(
                collective_id=0, has_side_effects=True, vmem_limit_bytes=56 * 1024 * 1024
            ),
        )(layer_input, proj_weight, ssd_input, log_decay.T, out_grad)
        grad_x, grad_log, grad_input, grad_weight = pl.pallas_call(
            store,
            out_shape=shapes,
            in_specs=[vmem] * 4,
            out_specs=(hbm,) * 4,
            scratch_shapes=[dma(4)],
            compiler_params=pltpu.CompilerParams(vmem_limit_bytes=1024 * 1024),
        )(*results)
        return grad_x, grad_log.T, grad_input, grad_weight

    return jax.shard_map(
        on_device,
        mesh=mesh,
        in_specs=(P("tm", "heads"),) * 5,
        out_specs=(P("tm", "heads"),) * 4,
        check_vma=False,
    )
```

```python
import jax
import jax.numpy as jnp
from jax import lax
from jax.experimental import pallas as pl
from jax.experimental.pallas import tpu as pltpu
from jax.sharding import PartitionSpec as P

N = 128
MESH = pl.DeviceIdType.MESH
HIGH = lax.Precision.HIGHEST
F32 = jnp.float32
BF16 = jnp.bfloat16


def nn(a, b, precision=None):
    return lax.dot_general(
        a, b, (((1,), (0,)), ((), ())), precision=precision, preferred_element_type=F32
    )


def nt(a, b, precision=None):
    return lax.dot_general(
        a, b, (((1,), (1,)), ((), ())), precision=precision, preferred_element_type=F32
    )


class Gather:
    def __init__(self, buf, send, recv, tm, me, heads_at):
        self.buf, self.send, self.recv = buf, send, recv
        self.tm, self.me, self.z = tm, me, heads_at
        self.chips = tm // 2
        self.chip, self.core = me // 2, lax.rem(me, 2)
        self.half_rows = buf.shape[1] // 2
        self.pending = []
        chip = self.chip
        if self.chips == 4:
            self.xn = chip + 1 - 2 * lax.rem(chip, 2)
            self.yn = lax.rem(chip + 2, 4)
            self.dg = 3 - chip

    def piece(self, slot, half):
        return self.buf.at[slot, pl.ds(half * self.half_rows, self.half_rows)]

    def copy(self, slot, half, chip, core, number):
        part = self.piece(slot, half)
        return pltpu.make_async_remote_copy(
            src_ref=part,
            dst_ref=part,
            send_sem=self.send.at[number],
            recv_sem=self.recv.at[slot, half],
            device_id=(chip * 2 + core, self.z),
            device_id_type=MESH,
        )

    def push(self, slot, half, chip, core):
        made = self.copy(slot, half, chip, core, len(self.pending))
        made.start()
        self.pending.append(made)

    def arrive(self, slot, half):
        self.copy(slot, half, self.chip, 1 - self.core, 0).wait_recv()

    def out(self):
        self.first()
        self.second()

    def first(self):
        me, core = self.me, self.core
        if self.chips == 4:
            self.push(me, 0, self.xn, core)
            self.push(me, 1, self.yn, core)
        else:
            for d in range(1, self.chips):
                self.push(me, 0, lax.rem(self.chip + d, self.chips), core)

    def second(self):
        me, core = self.me, self.core
        if self.chips == 4:
            self.push(me, 1, self.xn, core)
            self.push(me, 0, self.yn, core)
        else:
            for d in range(1, self.chips):
                self.push(me, 1, lax.rem(self.chip + d, self.chips), core)

    def relay(self):
        core = self.core
        if self.chips == 4:
            xs, ys = self.xn * 2 + core, self.yn * 2 + core
            self.arrive(xs, 0)
            self.push(xs, 0, self.yn, core)
            self.arrive(ys, 1)
            self.push(ys, 1, self.xn, core)

    def near(self):
        if self.chips != 4:
            return []
        xs, ys = self.xn * 2 + self.core, self.yn * 2 + self.core
        self.arrive(xs, 1)
        self.arrive(ys, 0)
        return [xs, ys]

    def far(self):
        if self.chips == 4:
            slots = [self.dg * 2 + self.core]
        else:
            slots = [
                lax.rem(self.chip + d, self.chips) * 2 + self.core for d in range(1, self.chips)
            ]
        for slot in slots:
            for half in range(2):
                self.arrive(slot, half)
        return slots

    def share(self, slots):
        for slot in slots:
            for half in range(2):
                self.push(slot, half, self.chip, 1 - self.core)

    def other(self, chip):
        for half in range(2):
            self.arrive(chip * 2 + 1 - self.core, half)

    def finish(self):
        for made in self.pending:
            made.wait_send()


def exchange(src, dst, send, recv, count, me, place):
    copies = []
    for d in range(1, count):
        to = lax.rem(me + d, count)
        copies.append(
            pltpu.make_async_remote_copy(
                src_ref=src(d, to),
                dst_ref=dst.at[me],
                send_sem=send.at[d],
                recv_sem=recv.at[me],
                device_id=place(to),
                device_id_type=MESH,
            )
        )
    for made in copies:
        made.start()
    return copies


def landed(dst, send, recv, slot, to):
    return pltpu.make_async_remote_copy(
        src_ref=dst.at[slot],
        dst_ref=dst.at[slot],
        send_sem=send.at[0],
        recv_sem=recv.at[slot],
        device_id=to,
        device_id_type=MESH,
    )


def kernel(
    tm, heads, members,
    li_hbm, w_hbm, x_hbm, log_hbm, dy_hbm,
    gx_ref, gl_ref, gi_ref, gw_ref,
    x_ref, dy_ref, log_ref,
    wbuf, libuf, dec, pbuf, bcr, st, sibst, agg, strecv, hin, gout, decay, dgx, lit, grecv, gall, grow,
    w_send, w_recv, li_send, li_recv, d_send, d_recv, p_send, p_recv, s_send, s_recv,
    g_send, g_recv, a_send, a_recv, in_sem,
):
    me = lax.axis_index("tm")
    z = lax.axis_index("heads")
    chips = tm // 2
    span = li_hbm.shape[0]
    heads_here = log_ref.shape[0]
    width = x_ref.shape[1]
    size = width // heads_here
    rows_w = w_hbm.shape[0]
    along = lambda to: (to, z)
    across_z = lambda to: (me, to)
    peer = (lax.rem(me + 1, tm), z)

    loads = [
        pltpu.make_async_copy(src, dst, in_sem.at[k])
        for k, (src, dst) in enumerate((
            (log_hbm, log_ref), (w_hbm, wbuf.at[me]), (x_hbm, x_ref), (dy_hbm, dy_ref),
            (li_hbm, libuf.at[me]),
        ))
    ]
    for made in loads:
        made.start()
    chip, core = me // 2, lax.rem(me, 2)
    barrier = pltpu.get_barrier_semaphore()
    for d in range(1, tm):
        pl.semaphore_signal(
            barrier, inc=1, device_id=along(lax.rem(me + d, tm)), device_id_type=MESH
        )
    for d in range(1, heads):
        pl.semaphore_signal(
            barrier, inc=1, device_id=across_z(lax.rem(z + d, heads)), device_id_type=MESH
        )
        pl.semaphore_signal(
            barrier,
            inc=1,
            device_id=(chip * 2 + 1 - core, lax.rem(z + d, heads)),
            device_id_type=MESH,
        )

    weights = Gather(wbuf, w_send, w_recv, tm, me, z)
    layer = Gather(libuf, li_send, li_recv, tm, me, z)
    started = []

    row = lax.broadcasted_iota(jnp.int32, (span, span), 0)
    col = lax.broadcasted_iota(jnp.int32, (span, span), 1)
    lower = (row >= col).astype(F32)
    upper = (row <= col).astype(F32)
    strict = (row > col).astype(F32)
    head_of = lax.broadcasted_iota(jnp.int32, (heads_here, width), 0) * size
    place = lax.broadcasted_iota(jnp.int32, (heads_here, width), 1)
    spread = ((place >= head_of) & (place < head_of + size)).astype(F32)
    loads[0].wait()
    sums_t = nn(log_ref[...], upper, HIGH)
    sums = sums_t.T
    wide = nn(sums, spread, HIGH)
    total = wide[span - 1 : span, :]
    dec[me] = jnp.broadcast_to(total, (8, width))
    loads[1].wait()
    pl.semaphore_wait(barrier, tm - 1 + 2 * (heads - 1))
    weights.out()
    loads[4].wait()
    layer.share([me])
    started += exchange(lambda d, to: dec.at[me], dec, d_send, d_recv, tm, me, along)
    loads[2].wait()
    loads[3].wait()
    from_start = jnp.exp(wide)
    to_end = jnp.exp(total - wide)
    x = x_ref[...]
    dy = dy_ref[...]
    x_end = to_end * x
    dy_start = from_start * dy
    x_end_t = x_end.T.astype(BF16)
    dy_start_t = dy_start.T.astype(BF16)
    x_end = x_end.astype(BF16)
    dy_start = dy_start.astype(BF16)
    lit[:, :span] = libuf[me].T
    x_half = x.astype(BF16)
    dy_half = dy.astype(BF16)

    dgx_sum = jnp.zeros((span, span), F32)

    def pairs_of(h, so_far):
        cut = slice(h * size, (h + 1) * size)
        gaps = sums_t[h : h + 1, :] - sums[:, h : h + 1]
        step = jnp.where(row <= col, jnp.exp(jnp.minimum(gaps, 0.0)), 0.0)
        pairs = step * nt(x_half[:, cut], dy_half[:, cut])
        decay[h] = step
        dgx[h] = pairs
        return so_far + pairs

    weights.relay()

    sent = []

    def project(slot):
        number = len(sent)
        k = slot // 2
        rows = nn(wbuf[slot], lit[...]).astype(BF16)
        pbuf[k, 0] = rows[:, :span]
        pbuf[k, 1] = rows[:, span:]
        part = lax.rem(k, 2)
        made = []
        for m in range(members):
            to = k // 2 * members + m
            for away in range(2):
                side = core if away == 0 else 1 - core
                made.append((to != z if away == 0 else None, pltpu.make_async_remote_copy(
                    src_ref=pbuf.at[k, away],
                    dst_ref=bcr.at[z, part, core],
                    send_sem=p_send.at[number, 2 * m + away],
                    recv_sem=p_recv.at[z, 2 * part + core],
                    device_id=(chip * 2 + side, to),
                    device_id_type=MESH,
                )))
        sent.append(made)
        for goes, copy in made:
            if goes is None:
                copy.start()
            else:
                pl.when(goes)(copy.start)

    layer.other(chip)
    lit[:, span:] = libuf[chip * 2 + 1 - core].T
    project(me)
    for h in range(heads_here):
        dgx_sum = pairs_of(h, dgx_sum)
    held = weights.near()
    for slot in held:
        project(slot)
    rest = weights.far()
    for slot in rest:
        project(slot)
    layer.first()
    group = z // members
    for part in range(2):
        bcr[z, part, core] = pbuf[2 * group + part, 0]

    def bc_landed(source, place):
        pltpu.make_async_remote_copy(
            src_ref=bcr.at[source, place // 2, lax.rem(place, 2)],
            dst_ref=bcr.at[source, place // 2, lax.rem(place, 2)],
            send_sem=p_send.at[0, 0],
            recv_sem=p_recv.at[source, place],
            device_id=peer,
            device_id_type=MESH,
        ).wait_recv()

    for part in range(2):
        bc_landed(z, 2 * part + 1 - core)
    for d in range(1, heads):
        for k in range(4):
            bc_landed(lax.rem(z + d, heads), k)
    bc = bcr[0].astype(F32)
    for k in range(1, heads):
        bc = bc + bcr[k].astype(F32)
    bc = bc.reshape(2, N, span)
    b_t = bc[0].astype(BF16)
    c_t = bc[1].astype(BF16)

    st[0] = nn(b_t, x_end).astype(BF16)
    st[1] = nn(c_t, dy_start).astype(BF16)
    half = width // 2
    sibling = chip * 2 + 1 - core

    def state_copy(src, dst, to, number, place):
        return pltpu.make_async_remote_copy(
            src_ref=src,
            dst_ref=dst,
            send_sem=s_send.at[number],
            recv_sem=s_recv.at[place],
            device_id=along(to),
            device_id_type=MESH,
        )

    swap = state_copy(st, sibst, sibling, 0, 2 * chip)
    swap.start()
    started.append(swap)
    for d in range(1, tm):
        landed(dec, d_send, d_recv, lax.rem(me + d, tm), peer).wait_recv()
    mine = pl.ds(pl.multiple_of(core * half, half), half)
    own_decay = jnp.exp(dec[me, 0:1, mine])
    sib_decay = jnp.exp(dec[sibling, 0:1, mine])
    one = jnp.ones_like(own_decay)
    first = core == 0
    swap.wait_recv()
    agg[0] = (
        jnp.where(first, sib_decay, one) * st[0, :, mine].astype(F32)
        + jnp.where(first, one, own_decay) * sibst[0, :, mine].astype(F32)
    ).astype(BF16)
    agg[1] = (
        jnp.where(first, one, sib_decay) * st[1, :, mine].astype(F32)
        + jnp.where(first, own_decay, one) * sibst[1, :, mine].astype(F32)
    ).astype(BF16)
    for d in range(1, chips):
        to = lax.rem(chip + d, chips) * 2 + core
        made = state_copy(
            agg.at[(chip + d) // chips], strecv.at[me], to, d, me
        )
        made.start()
        started.append(made)
    weights.share([me] + held + rest)
    b = bc[0].T.astype(BF16)
    c = bc[1].T.astype(BF16)

    cb = nn(b, c_t)
    after = []
    before = []
    for h in range(heads_here):
        cut = slice(h * size, (h + 1) * size)
        weight = decay[h] * cb
        gx_ref[:, cut] = nn(weight.astype(BF16), dy_half[:, cut])
        product = dgx[h] * cb
        after.append(jnp.sum(product, axis=1, keepdims=True))
        before.append(jnp.sum(product, axis=0, keepdims=True))
    before = jnp.concatenate(before, axis=0)
    after = jnp.concatenate(after, axis=1)
    grad_b = nn(c_t, dgx_sum.T.astype(BF16))
    grad_c = nn(b_t, dgx_sum.astype(BF16))
    inside = nn(strict, after, HIGH) - nt(strict, before, HIGH)

    for d in range(1, chips):
        slot = lax.rem(chip + d, chips) * 2 + core
        landed(strecv, s_send, s_recv, slot, peer).wait_recv()
        made = state_copy(strecv.at[slot], strecv.at[slot], sibling, chips - 1 + d, slot)
        made.start()
        started.append(made)
    layer.second()
    layer.relay()
    for d in range(1, chips):
        slot = lax.rem(chip + d, chips) * 2 + 1 - core
        landed(strecv, s_send, s_recv, slot, peer).wait_recv()
    hin[...] = jnp.zeros_like(hin)
    gout[...] = jnp.zeros_like(gout)

    def fold(ref, q):
        decays = jnp.exp(dec[2 * q][0:1, :] + dec[2 * q + 1][0:1, :])
        for k in range(2):
            cut = slice(k * half, (k + 1) * half)
            ref[:, cut] = ref[:, cut] * decays[:, cut] + strecv[2 * q + k].astype(F32)

    def forward(q, _):
        fold(hin, q)
        return 0

    def backward(k, _):
        fold(gout, chips - 1 - k)
        return 0

    def fold_sibling(ref, part):
        ref[...] = ref[...] * jnp.exp(dec[sibling][0:1, :]) + sibst[part].astype(F32)

    def send_grad(part, value):
        grecv[z, part] = value.astype(BF16)
        copies = []
        for d in range(1, heads):
            copies.append(pltpu.make_async_remote_copy(
                src_ref=grecv.at[z, part],
                dst_ref=grecv.at[z, part],
                send_sem=g_send.at[d, part],
                recv_sem=g_recv.at[z, part],
                device_id=across_z(lax.rem(z + d, heads)),
                device_id_type=MESH,
            ))
        for made in copies:
            made.start()
        return copies

    lax.fori_loop(0, chips - 1 - chip, backward, 0)
    pl.when(core == 0)(lambda: fold_sibling(gout, 1))
    grad = gout[...]
    grad_half = grad.astype(BF16)
    started += send_grad(0, grad_b + nn(grad_half, x_end_t))
    lax.fori_loop(0, chip, forward, 0)
    pl.when(core == 1)(lambda: fold_sibling(hin, 0))
    state = hin[...]
    state_half = state.astype(BF16)
    started += send_grad(1, grad_c + nn(state_half, dy_start_t))

    from_end = to_end * nn(b, grad_half)
    gx_ref[...] += from_end
    earlier = nt(from_start * nn(c, state_half) * dy, spread, HIGH)
    later = nt(from_end * x, spread, HIGH)
    through = jnp.sum(grad * state, axis=0, keepdims=True) * jnp.exp(total)
    through = nt(jnp.broadcast_to(through, (8, width)), spread, HIGH)
    gl_ref[...] = (
        inside + nn(upper, earlier, HIGH) + nn(strict, later, HIGH) + through[0:1, :]
    ).T

    for d in range(1, heads):
        other = lax.rem(z + d, heads)
        for part in range(2):
            pltpu.make_async_remote_copy(
                src_ref=grecv.at[other, part],
                dst_ref=grecv.at[other, part],
                send_sem=g_send.at[0, 0],
                recv_sem=g_recv.at[other, part],
                device_id=peer,
                device_id_type=MESH,
            ).wait_recv()
    turned = []
    for g in range(heads // members):
        for part in range(2):
            acc = grecv[g * members, part].astype(F32)
            for k in range(1, members):
                acc = acc + grecv[g * members + k, part].astype(F32)
            piece = acc.astype(BF16)
            first = (2 * g + part) * N // rows_w
            for k in range(N // rows_w):
                gall[first + k] = piece[k * rows_w : (k + 1) * rows_w]
            turned.append(piece)
    last = exchange(lambda d, to: gall.at[to], grow, a_send, a_recv, tm, me, along)
    grow[me] = gall[me]
    layer.share(layer.near())
    layer.share(layer.far())
    grad_bc = jnp.concatenate([k.astype(F32).T.astype(BF16) for k in turned], axis=1)
    for made in started:
        made.wait_send()
    for made in sent:
        for goes, copy in made:
            if goes is None:
                copy.wait_send()
            else:
                pl.when(goes)(copy.wait_send)
    for k in range(chips):
        weights.other(k)
    weights.finish()
    gi_ref[...] = nn(grad_bc, wbuf[...].reshape(tm * rows_w, wbuf.shape[2])).astype(BF16)

    for d in range(1, chips):
        layer.other(lax.rem(layer.chip + d, chips))
    for d in range(1, tm):
        landed(grow, a_send, a_recv, lax.rem(me + d, tm), peer).wait_recv()
    rows = jnp.concatenate([grow[k] for k in range(tm)], axis=1)
    gw_ref[...] = nn(rows, libuf[...].reshape(tm * span, libuf.shape[2]))

    for made in last:
        made.wait_send()
    layer.finish()


def store(*refs):
    sems = refs[-1]
    count = (len(refs) - 1) // 2
    copies = [pltpu.make_async_copy(refs[k], refs[count + k], sems.at[k]) for k in range(count)]
    for made in copies:
        made.start()
    for made in copies:
        made.wait()


def solution(mesh):
    tm = mesh.shape["tm"]
    heads = mesh.shape["heads"]
    chips = tm // 2

    def on_device(layer_input, proj_weight, ssd_input, log_decay, out_grad):
        span, depth = layer_input.shape
        rows_w = proj_weight.shape[0]
        heads_here = log_decay.shape[1]
        width = ssd_input.shape[1]
        groups = rows_w * tm // (2 * N)
        members = heads // groups
        copies = 14 if chips == 4 else 4 * (chips - 1) + 2
        dma = lambda *shape: pltpu.SemaphoreType.DMA(shape)
        vmem = pl.BlockSpec(memory_space=pltpu.VMEM)
        hbm = pl.BlockSpec(memory_space=pltpu.HBM)
        shapes = (
            jax.ShapeDtypeStruct((span, width), F32),
            jax.ShapeDtypeStruct((heads_here, span), F32),
            jax.ShapeDtypeStruct((span, depth), BF16),
            jax.ShapeDtypeStruct((rows_w, depth), F32),
        )

        def body(*refs):
            kernel(tm, heads, members, *refs)

        results = pl.pallas_call(
            body,
            out_shape=tuple(pltpu.VMEM(k.shape, k.dtype) for k in shapes),
            in_specs=[hbm] * 5,
            out_specs=(vmem,) * 4,
            scratch_shapes=[
                pltpu.VMEM((span, width), F32),
                pltpu.VMEM((span, width), F32),
                pltpu.VMEM((heads_here, span), F32),
                pltpu.VMEM((tm, rows_w, depth), BF16),
                pltpu.VMEM((tm, span, depth), BF16),
                pltpu.VMEM((tm, 8, width), F32),
                pltpu.VMEM((chips, 2, rows_w, span), BF16),
                pltpu.VMEM((heads, 2, 2, rows_w, span), BF16),
                pltpu.VMEM((2, N, width), BF16),
                pltpu.VMEM((2, N, width), BF16),
                pltpu.VMEM((2, N, width // 2), BF16),
                pltpu.VMEM((tm, N, width // 2), BF16),
                pltpu.VMEM((N, width), F32),
                pltpu.VMEM((N, width), F32),
                pltpu.VMEM((heads_here, span, span), F32),
                pltpu.VMEM((heads_here, span, span), F32),
                pltpu.VMEM((depth, 2 * span), BF16),
                pltpu.VMEM((heads, 2, N, span), BF16),
                pltpu.VMEM((tm, rows_w, span), BF16),
                pltpu.VMEM((tm, rows_w, span), BF16),
                dma(copies), dma(tm, 2),
                dma(copies), dma(tm, 2),
                dma(tm), dma(tm),
                dma(chips, 2 * members), dma(heads, 4),
                dma(tm), dma(tm),
                dma(heads, 2), dma(heads, 2),
                dma(tm), dma(tm),
                dma(5),
            ],
            compiler_params=pltpu.CompilerParams(
                collective_id=0, has_side_effects=True, vmem_limit_bytes=56 * 1024 * 1024
            ),
        )(layer_input, proj_weight, ssd_input, log_decay.T, out_grad)
        grad_x, grad_log, grad_input, grad_weight = pl.pallas_call(
            store,
            out_shape=shapes,
            in_specs=[vmem] * 4,
            out_specs=(hbm,) * 4,
            scratch_shapes=[dma(4)],
            compiler_params=pltpu.CompilerParams(vmem_limit_bytes=1024 * 1024),
        )(*results)
        return grad_x, grad_log.T, grad_input, grad_weight

    return jax.shard_map(
        on_device,
        mesh=mesh,
        in_specs=(P("tm", "heads"),) * 5,
        out_specs=(P("tm", "heads"),) * 4,
        check_vma=False,
    )
```

```python
import jax
import jax.numpy as jnp
from jax import lax
from jax.experimental import pallas as pl
from jax.experimental.pallas import tpu as pltpu
from jax.sharding import PartitionSpec as P

N = 128
MESH = pl.DeviceIdType.MESH
HIGH = lax.Precision.HIGHEST
F32 = jnp.float32
BF16 = jnp.bfloat16


def nn(a, b, precision=None):
    return lax.dot_general(
        a, b, (((1,), (0,)), ((), ())), precision=precision, preferred_element_type=F32
    )


def nt(a, b, precision=None):
    return lax.dot_general(
        a, b, (((1,), (1,)), ((), ())), precision=precision, preferred_element_type=F32
    )


class Gather:
    def __init__(self, buf, send, recv, tm, me, heads_at):
        self.buf, self.send, self.recv = buf, send, recv
        self.tm, self.me, self.z = tm, me, heads_at
        self.chips = tm // 2
        self.chip, self.core = me // 2, lax.rem(me, 2)
        self.half_rows = buf.shape[1] // 2
        self.pending = []
        chip = self.chip
        if self.chips == 4:
            self.xn = chip + 1 - 2 * lax.rem(chip, 2)
            self.yn = lax.rem(chip + 2, 4)
            self.dg = 3 - chip

    def piece(self, slot, half, quarter):
        if quarter is None:
            return self.buf.at[slot, pl.ds(half * self.half_rows, self.half_rows)]
        rows = self.half_rows // 2
        return self.buf.at[slot, pl.ds((2 * half + quarter) * rows, rows)]

    def copy(self, slot, half, chip, core, number, quarter=None):
        part = self.piece(slot, half, quarter)
        return pltpu.make_async_remote_copy(
            src_ref=part,
            dst_ref=part,
            send_sem=self.send.at[number],
            recv_sem=self.recv.at[slot, half],
            device_id=(chip * 2 + core, self.z),
            device_id_type=MESH,
        )

    def push(self, slot, half, chip, core, quarter=None):
        made = self.copy(slot, half, chip, core, len(self.pending), quarter)
        made.start()
        self.pending.append(made)

    def arrive(self, slot, half):
        self.copy(slot, half, self.chip, 1 - self.core, 0).wait_recv()

    def out(self):
        self.first()
        self.second()

    def first(self):
        me, core = self.me, self.core
        if self.chips == 4:
            self.push(me, 0, self.xn, core)
            self.push(me, 1, self.yn, core)
        else:
            for d in range(1, self.chips):
                self.push(me, 0, lax.rem(self.chip + d, self.chips), core)

    def second(self, quarter=None):
        me, core = self.me, self.core
        if self.chips == 4:
            self.push(me, 1, self.xn, core, quarter)
            self.push(me, 0, self.yn, core, quarter)
        else:
            for d in range(1, self.chips):
                self.push(me, 1, lax.rem(self.chip + d, self.chips), core, quarter)

    def relay(self):
        core = self.core
        if self.chips == 4:
            xs, ys = self.xn * 2 + core, self.yn * 2 + core
            self.arrive(xs, 0)
            self.push(xs, 0, self.yn, core)
            self.arrive(ys, 1)
            self.push(ys, 1, self.xn, core)

    def near(self):
        if self.chips != 4:
            return []
        xs, ys = self.xn * 2 + self.core, self.yn * 2 + self.core
        self.arrive(xs, 1)
        self.arrive(ys, 0)
        return [xs, ys]

    def far(self):
        if self.chips == 4:
            slots = [self.dg * 2 + self.core]
        else:
            slots = [
                lax.rem(self.chip + d, self.chips) * 2 + self.core for d in range(1, self.chips)
            ]
        for slot in slots:
            for half in range(2):
                self.arrive(slot, half)
        return slots

    def share(self, slots):
        for slot in slots:
            for half in range(2):
                self.push(slot, half, self.chip, 1 - self.core)

    def other(self, chip):
        for half in range(2):
            self.arrive(chip * 2 + 1 - self.core, half)

    def finish(self):
        for made in self.pending:
            made.wait_send()


def exchange(src, dst, send, recv, count, me, place):
    copies = []
    for d in range(1, count):
        to = lax.rem(me + d, count)
        copies.append(
            pltpu.make_async_remote_copy(
                src_ref=src(d, to),
                dst_ref=dst.at[me],
                send_sem=send.at[d],
                recv_sem=recv.at[me],
                device_id=place(to),
                device_id_type=MESH,
            )
        )
    for made in copies:
        made.start()
    return copies


def landed(dst, send, recv, slot, to):
    return pltpu.make_async_remote_copy(
        src_ref=dst.at[slot],
        dst_ref=dst.at[slot],
        send_sem=send.at[0],
        recv_sem=recv.at[slot],
        device_id=to,
        device_id_type=MESH,
    )


def kernel(
    tm, heads, members,
    li_hbm, w_hbm, x_hbm, log_hbm, dy_hbm,
    gx_ref, gl_ref, gi_ref, gw_ref,
    x_ref, dy_ref, log_ref,
    wbuf, libuf, dec, pbuf, bcr, st, sibst, agg, strecv, hin, gout, decay, dgx, lit, grecv, gall, grow,
    w_send, w_recv, li_send, li_recv, d_send, d_recv, p_send, p_recv, s_send, s_recv,
    g_send, g_recv, a_send, a_recv, in_sem,
):
    me = lax.axis_index("tm")
    z = lax.axis_index("heads")
    chips = tm // 2
    span = li_hbm.shape[0]
    heads_here = log_ref.shape[0]
    width = x_ref.shape[1]
    size = width // heads_here
    rows_w = w_hbm.shape[0]
    along = lambda to: (to, z)
    across_z = lambda to: (me, to)
    peer = (lax.rem(me + 1, tm), z)

    loads = [
        pltpu.make_async_copy(src, dst, in_sem.at[k])
        for k, (src, dst) in enumerate((
            (log_hbm, log_ref), (w_hbm, wbuf.at[me]), (x_hbm, x_ref), (dy_hbm, dy_ref),
            (li_hbm, libuf.at[me]),
        ))
    ]
    for made in loads:
        made.start()
    chip, core = me // 2, lax.rem(me, 2)
    barrier = pltpu.get_barrier_semaphore()
    for d in range(1, tm):
        pl.semaphore_signal(
            barrier, inc=1, device_id=along(lax.rem(me + d, tm)), device_id_type=MESH
        )
    for d in range(1, heads):
        pl.semaphore_signal(
            barrier, inc=1, device_id=across_z(lax.rem(z + d, heads)), device_id_type=MESH
        )
        pl.semaphore_signal(
            barrier,
            inc=1,
            device_id=(chip * 2 + 1 - core, lax.rem(z + d, heads)),
            device_id_type=MESH,
        )

    weights = Gather(wbuf, w_send, w_recv, tm, me, z)
    layer = Gather(libuf, li_send, li_recv, tm, me, z)
    started = []

    row = lax.broadcasted_iota(jnp.int32, (span, span), 0)
    col = lax.broadcasted_iota(jnp.int32, (span, span), 1)
    lower = (row >= col).astype(F32)
    upper = (row <= col).astype(F32)
    strict = (row > col).astype(F32)
    head_of = lax.broadcasted_iota(jnp.int32, (heads_here, width), 0) * size
    place = lax.broadcasted_iota(jnp.int32, (heads_here, width), 1)
    spread = ((place >= head_of) & (place < head_of + size)).astype(F32)
    loads[0].wait()
    sums_t = nn(log_ref[...], upper, HIGH)
    sums = sums_t.T
    wide = nn(sums, spread, HIGH)
    total = wide[span - 1 : span, :]
    dec[me] = jnp.broadcast_to(total, (8, width))
    loads[1].wait()
    pl.semaphore_wait(barrier, tm - 1 + 2 * (heads - 1))
    weights.out()
    loads[4].wait()
    layer.share([me])
    started += exchange(lambda d, to: dec.at[me], dec, d_send, d_recv, tm, me, along)
    loads[2].wait()
    loads[3].wait()
    from_start = jnp.exp(wide)
    to_end = jnp.exp(total - wide)
    x = x_ref[...]
    dy = dy_ref[...]
    x_end = to_end * x
    dy_start = from_start * dy
    x_end_t = x_end.T.astype(BF16)
    dy_start_t = dy_start.T.astype(BF16)
    x_end = x_end.astype(BF16)
    dy_start = dy_start.astype(BF16)
    lit[:, :span] = libuf[me].T
    x_half = x.astype(BF16)
    dy_half = dy.astype(BF16)

    dgx_sum = jnp.zeros((span, span), F32)

    def pairs_of(h, so_far):
        cut = slice(h * size, (h + 1) * size)
        gaps = sums_t[h : h + 1, :] - sums[:, h : h + 1]
        step = jnp.where(row <= col, jnp.exp(jnp.minimum(gaps, 0.0)), 0.0)
        pairs = step * nt(x_half[:, cut], dy_half[:, cut])
        decay[h] = step
        dgx[h] = pairs
        return so_far + pairs

    weights.relay()

    sent = []

    def project(slot):
        number = len(sent)
        k = slot // 2
        rows = nn(wbuf[slot], lit[...]).astype(BF16)
        pbuf[k, 0] = rows[:, :span]
        pbuf[k, 1] = rows[:, span:]
        part = lax.rem(k, 2)
        made = []
        for m in range(members):
            to = k // 2 * members + m
            for away in range(2):
                side = core if away == 0 else 1 - core
                made.append((to != z if away == 0 else None, pltpu.make_async_remote_copy(
                    src_ref=pbuf.at[k, away],
                    dst_ref=bcr.at[z, part, core],
                    send_sem=p_send.at[number, 2 * m + away],
                    recv_sem=p_recv.at[z, 2 * part + core],
                    device_id=(chip * 2 + side, to),
                    device_id_type=MESH,
                )))
        sent.append(made)
        for goes, copy in made:
            if goes is None:
                copy.start()
            else:
                pl.when(goes)(copy.start)

    layer.other(chip)
    lit[:, span:] = libuf[chip * 2 + 1 - core].T
    project(me)
    for h in range(heads_here):
        dgx_sum = pairs_of(h, dgx_sum)
    held = weights.near()
    for slot in held:
        project(slot)
    rest = weights.far()
    for slot in rest:
        project(slot)
    layer.first()
    group = z // members
    for part in range(2):
        bcr[z, part, core] = pbuf[2 * group + part, 0]

    def bc_landed(source, place):
        pltpu.make_async_remote_copy(
            src_ref=bcr.at[source, place // 2, lax.rem(place, 2)],
            dst_ref=bcr.at[source, place // 2, lax.rem(place, 2)],
            send_sem=p_send.at[0, 0],
            recv_sem=p_recv.at[source, place],
            device_id=peer,
            device_id_type=MESH,
        ).wait_recv()

    for part in range(2):
        bc_landed(z, 2 * part + 1 - core)
    for d in range(1, heads):
        for k in range(4):
            bc_landed(lax.rem(z + d, heads), k)
    bc = bcr[0].astype(F32)
    for k in range(1, heads):
        bc = bc + bcr[k].astype(F32)
    bc = bc.reshape(2, N, span)
    b_t = bc[0].astype(BF16)
    c_t = bc[1].astype(BF16)

    st[0] = nn(b_t, x_end).astype(BF16)
    st[1] = nn(c_t, dy_start).astype(BF16)
    half = width // 2
    sibling = chip * 2 + 1 - core

    def state_copy(src, dst, to, number, place):
        return pltpu.make_async_remote_copy(
            src_ref=src,
            dst_ref=dst,
            send_sem=s_send.at[number],
            recv_sem=s_recv.at[place],
            device_id=along(to),
            device_id_type=MESH,
        )

    swap = state_copy(st, sibst, sibling, 0, 2 * chip)
    swap.start()
    layer.second(0)
    started.append(swap)
    for d in range(1, tm):
        landed(dec, d_send, d_recv, lax.rem(me + d, tm), peer).wait_recv()
    mine = pl.ds(pl.multiple_of(core * half, half), half)
    own_decay = jnp.exp(dec[me, 0:1, mine])
    sib_decay = jnp.exp(dec[sibling, 0:1, mine])
    one = jnp.ones_like(own_decay)
    first = core == 0
    swap.wait_recv()
    agg[0] = (
        jnp.where(first, sib_decay, one) * st[0, :, mine].astype(F32)
        + jnp.where(first, one, own_decay) * sibst[0, :, mine].astype(F32)
    ).astype(BF16)
    agg[1] = (
        jnp.where(first, one, sib_decay) * st[1, :, mine].astype(F32)
        + jnp.where(first, own_decay, one) * sibst[1, :, mine].astype(F32)
    ).astype(BF16)
    for d in range(1, chips):
        to = lax.rem(chip + d, chips) * 2 + core
        made = state_copy(
            agg.at[(chip + d) // chips], strecv.at[me], to, d, me
        )
        made.start()
        started.append(made)
    weights.share([me] + held + rest)
    b = bc[0].T.astype(BF16)
    c = bc[1].T.astype(BF16)

    cb = nn(b, c_t)
    after = []
    before = []
    for h in range(heads_here):
        cut = slice(h * size, (h + 1) * size)
        weight = decay[h] * cb
        gx_ref[:, cut] = nn(weight.astype(BF16), dy_half[:, cut])
        product = dgx[h] * cb
        after.append(jnp.sum(product, axis=1, keepdims=True))
        before.append(jnp.sum(product, axis=0, keepdims=True))
    before = jnp.concatenate(before, axis=0)
    after = jnp.concatenate(after, axis=1)
    grad_b = nn(c_t, dgx_sum.T.astype(BF16))
    grad_c = nn(b_t, dgx_sum.astype(BF16))
    inside = nn(strict, after, HIGH) - nt(strict, before, HIGH)

    for d in range(1, chips):
        slot = lax.rem(chip + d, chips) * 2 + core
        landed(strecv, s_send, s_recv, slot, peer).wait_recv()
        made = state_copy(strecv.at[slot], strecv.at[slot], sibling, chips - 1 + d, slot)
        made.start()
        started.append(made)
    layer.relay()
    layer.second(1)
    for d in range(1, chips):
        slot = lax.rem(chip + d, chips) * 2 + 1 - core
        landed(strecv, s_send, s_recv, slot, peer).wait_recv()
    hin[...] = jnp.zeros_like(hin)
    gout[...] = jnp.zeros_like(gout)

    def fold(ref, q):
        decays = jnp.exp(dec[2 * q][0:1, :] + dec[2 * q + 1][0:1, :])
        for k in range(2):
            cut = slice(k * half, (k + 1) * half)
            ref[:, cut] = ref[:, cut] * decays[:, cut] + strecv[2 * q + k].astype(F32)

    def forward(q, _):
        fold(hin, q)
        return 0

    def backward(k, _):
        fold(gout, chips - 1 - k)
        return 0

    def fold_sibling(ref, part):
        ref[...] = ref[...] * jnp.exp(dec[sibling][0:1, :]) + sibst[part].astype(F32)

    def send_grad(part, value):
        grecv[z, part] = value.astype(BF16)
        copies = []
        for d in range(1, heads):
            copies.append(pltpu.make_async_remote_copy(
                src_ref=grecv.at[z, part],
                dst_ref=grecv.at[z, part],
                send_sem=g_send.at[d, part],
                recv_sem=g_recv.at[z, part],
                device_id=across_z(lax.rem(z + d, heads)),
                device_id_type=MESH,
            ))
        for made in copies:
            made.start()
        return copies

    lax.fori_loop(0, chips - 1 - chip, backward, 0)
    pl.when(core == 0)(lambda: fold_sibling(gout, 1))
    grad = gout[...]
    grad_half = grad.astype(BF16)
    started += send_grad(0, grad_b + nn(grad_half, x_end_t))
    lax.fori_loop(0, chip, forward, 0)
    pl.when(core == 1)(lambda: fold_sibling(hin, 0))
    state = hin[...]
    state_half = state.astype(BF16)
    started += send_grad(1, grad_c + nn(state_half, dy_start_t))

    from_end = to_end * nn(b, grad_half)
    gx_ref[...] += from_end
    earlier = nt(from_start * nn(c, state_half) * dy, spread, HIGH)
    later = nt(from_end * x, spread, HIGH)
    through = jnp.sum(grad * state, axis=0, keepdims=True) * jnp.exp(total)
    through = nt(jnp.broadcast_to(through, (8, width)), spread, HIGH)
    gl_ref[...] = (
        inside + nn(upper, earlier, HIGH) + nn(strict, later, HIGH) + through[0:1, :]
    ).T

    for d in range(1, heads):
        other = lax.rem(z + d, heads)
        for part in range(2):
            pltpu.make_async_remote_copy(
                src_ref=grecv.at[other, part],
                dst_ref=grecv.at[other, part],
                send_sem=g_send.at[0, 0],
                recv_sem=g_recv.at[other, part],
                device_id=peer,
                device_id_type=MESH,
            ).wait_recv()
    turned = []
    for g in range(heads // members):
        for part in range(2):
            acc = grecv[g * members, part].astype(F32)
            for k in range(1, members):
                acc = acc + grecv[g * members + k, part].astype(F32)
            piece = acc.astype(BF16)
            first = (2 * g + part) * N // rows_w
            for k in range(N // rows_w):
                gall[first + k] = piece[k * rows_w : (k + 1) * rows_w]
            turned.append(piece)
    last = exchange(lambda d, to: gall.at[to], grow, a_send, a_recv, tm, me, along)
    grow[me] = gall[me]
    layer.share(layer.near())
    layer.share(layer.far())
    grad_bc = jnp.concatenate([k.astype(F32).T.astype(BF16) for k in turned], axis=1)
    for made in started:
        made.wait_send()
    for made in sent:
        for goes, copy in made:
            if goes is None:
                copy.wait_send()
            else:
                pl.when(goes)(copy.wait_send)
    for k in range(chips):
        weights.other(k)
    weights.finish()
    gi_ref[...] = nn(grad_bc, wbuf[...].reshape(tm * rows_w, wbuf.shape[2])).astype(BF16)

    for d in range(1, chips):
        layer.other(lax.rem(layer.chip + d, chips))
    for d in range(1, tm):
        landed(grow, a_send, a_recv, lax.rem(me + d, tm), peer).wait_recv()
    rows = jnp.concatenate([grow[k] for k in range(tm)], axis=1)
    gw_ref[...] = nn(rows, libuf[...].reshape(tm * span, libuf.shape[2]))

    for made in last:
        made.wait_send()
    layer.finish()


def store(*refs):
    sems = refs[-1]
    count = (len(refs) - 1) // 2
    copies = [pltpu.make_async_copy(refs[k], refs[count + k], sems.at[k]) for k in range(count)]
    for made in copies:
        made.start()
    for made in copies:
        made.wait()


def solution(mesh):
    tm = mesh.shape["tm"]
    heads = mesh.shape["heads"]
    chips = tm // 2

    def on_device(layer_input, proj_weight, ssd_input, log_decay, out_grad):
        span, depth = layer_input.shape
        rows_w = proj_weight.shape[0]
        heads_here = log_decay.shape[1]
        width = ssd_input.shape[1]
        groups = rows_w * tm // (2 * N)
        members = heads // groups
        copies = 14 if chips == 4 else 4 * (chips - 1) + 2
        dma = lambda *shape: pltpu.SemaphoreType.DMA(shape)
        vmem = pl.BlockSpec(memory_space=pltpu.VMEM)
        hbm = pl.BlockSpec(memory_space=pltpu.HBM)
        shapes = (
            jax.ShapeDtypeStruct((span, width), F32),
            jax.ShapeDtypeStruct((heads_here, span), F32),
            jax.ShapeDtypeStruct((span, depth), BF16),
            jax.ShapeDtypeStruct((rows_w, depth), F32),
        )

        def body(*refs):
            kernel(tm, heads, members, *refs)

        results = pl.pallas_call(
            body,
            out_shape=tuple(pltpu.VMEM(k.shape, k.dtype) for k in shapes),
            in_specs=[hbm] * 5,
            out_specs=(vmem,) * 4,
            scratch_shapes=[
                pltpu.VMEM((span, width), F32),
                pltpu.VMEM((span, width), F32),
                pltpu.VMEM((heads_here, span), F32),
                pltpu.VMEM((tm, rows_w, depth), BF16),
                pltpu.VMEM((tm, span, depth), BF16),
                pltpu.VMEM((tm, 8, width), F32),
                pltpu.VMEM((chips, 2, rows_w, span), BF16),
                pltpu.VMEM((heads, 2, 2, rows_w, span), BF16),
                pltpu.VMEM((2, N, width), BF16),
                pltpu.VMEM((2, N, width), BF16),
                pltpu.VMEM((2, N, width // 2), BF16),
                pltpu.VMEM((tm, N, width // 2), BF16),
                pltpu.VMEM((N, width), F32),
                pltpu.VMEM((N, width), F32),
                pltpu.VMEM((heads_here, span, span), F32),
                pltpu.VMEM((heads_here, span, span), F32),
                pltpu.VMEM((depth, 2 * span), BF16),
                pltpu.VMEM((heads, 2, N, span), BF16),
                pltpu.VMEM((tm, rows_w, span), BF16),
                pltpu.VMEM((tm, rows_w, span), BF16),
                dma(copies), dma(tm, 2),
                dma(copies + chips), dma(tm, 2),
                dma(tm), dma(tm),
                dma(chips, 2 * members), dma(heads, 4),
                dma(tm), dma(tm),
                dma(heads, 2), dma(heads, 2),
                dma(tm), dma(tm),
                dma(5),
            ],
            compiler_params=pltpu.CompilerParams(
                collective_id=0, has_side_effects=True, vmem_limit_bytes=56 * 1024 * 1024
            ),
        )(layer_input, proj_weight, ssd_input, log_decay.T, out_grad)
        grad_x, grad_log, grad_input, grad_weight = pl.pallas_call(
            store,
            out_shape=shapes,
            in_specs=[vmem] * 4,
            out_specs=(hbm,) * 4,
            scratch_shapes=[dma(4)],
            compiler_params=pltpu.CompilerParams(vmem_limit_bytes=1024 * 1024),
        )(*results)
        return grad_x, grad_log.T, grad_input, grad_weight

    return jax.shard_map(
        on_device,
        mesh=mesh,
        in_specs=(P("tm", "heads"),) * 5,
        out_specs=(P("tm", "heads"),) * 4,
        check_vma=False,
    )
```

```python
import jax
import jax.numpy as jnp
from jax import lax
from jax.experimental import pallas as pl
from jax.experimental.pallas import tpu as pltpu
from jax.sharding import PartitionSpec as P

N = 128
MESH = pl.DeviceIdType.MESH
HIGH = lax.Precision.HIGHEST
F32 = jnp.float32
BF16 = jnp.bfloat16


def nn(a, b, precision=None):
    return lax.dot_general(
        a, b, (((1,), (0,)), ((), ())), precision=precision, preferred_element_type=F32
    )


def nt(a, b, precision=None):
    return lax.dot_general(
        a, b, (((1,), (1,)), ((), ())), precision=precision, preferred_element_type=F32
    )


class Gather:
    def __init__(self, buf, send, recv, tm, me, heads_at):
        self.buf, self.send, self.recv = buf, send, recv
        self.tm, self.me, self.z = tm, me, heads_at
        self.chips = tm // 2
        self.chip, self.core = me // 2, lax.rem(me, 2)
        self.half_rows = buf.shape[1] // 2
        self.pending = []
        chip = self.chip
        if self.chips == 4:
            self.xn = chip + 1 - 2 * lax.rem(chip, 2)
            self.yn = lax.rem(chip + 2, 4)
            self.dg = 3 - chip

    def piece(self, slot, half, quarter):
        if quarter is None:
            return self.buf.at[slot, pl.ds(half * self.half_rows, self.half_rows)]
        rows = self.half_rows // 2
        return self.buf.at[slot, pl.ds((2 * half + quarter) * rows, rows)]

    def copy(self, slot, half, chip, core, number, quarter=None):
        part = self.piece(slot, half, quarter)
        return pltpu.make_async_remote_copy(
            src_ref=part,
            dst_ref=part,
            send_sem=self.send.at[number],
            recv_sem=self.recv.at[slot, half],
            device_id=(chip * 2 + core, self.z),
            device_id_type=MESH,
        )

    def push(self, slot, half, chip, core, quarter=None):
        made = self.copy(slot, half, chip, core, len(self.pending), quarter)
        made.start()
        self.pending.append(made)

    def arrive(self, slot, half):
        self.copy(slot, half, self.chip, 1 - self.core, 0).wait_recv()

    def out(self):
        self.first()
        self.second()

    def first(self):
        me, core = self.me, self.core
        if self.chips == 4:
            self.push(me, 0, self.xn, core)
            self.push(me, 1, self.yn, core)
        else:
            for d in range(1, self.chips):
                self.push(me, 0, lax.rem(self.chip + d, self.chips), core)

    def second(self, quarter=None):
        me, core = self.me, self.core
        if self.chips == 4:
            self.push(me, 1, self.xn, core, quarter)
            self.push(me, 0, self.yn, core, quarter)
        else:
            for d in range(1, self.chips):
                self.push(me, 1, lax.rem(self.chip + d, self.chips), core, quarter)

    def relay(self):
        core = self.core
        if self.chips == 4:
            xs, ys = self.xn * 2 + core, self.yn * 2 + core
            self.arrive(xs, 0)
            self.push(xs, 0, self.yn, core)
            self.arrive(ys, 1)
            self.push(ys, 1, self.xn, core)

    def near(self):
        if self.chips != 4:
            return []
        xs, ys = self.xn * 2 + self.core, self.yn * 2 + self.core
        self.arrive(xs, 1)
        self.arrive(ys, 0)
        return [xs, ys]

    def far(self):
        if self.chips == 4:
            slots = [self.dg * 2 + self.core]
        else:
            slots = [
                lax.rem(self.chip + d, self.chips) * 2 + self.core for d in range(1, self.chips)
            ]
        for slot in slots:
            for half in range(2):
                self.arrive(slot, half)
        return slots

    def share(self, slots):
        for slot in slots:
            for half in range(2):
                self.push(slot, half, self.chip, 1 - self.core)

    def other(self, chip):
        for half in range(2):
            self.arrive(chip * 2 + 1 - self.core, half)

    def finish(self):
        for made in self.pending:
            made.wait_send()


def exchange(src, dst, send, recv, count, me, place):
    copies = []
    for d in range(1, count):
        to = lax.rem(me + d, count)
        copies.append(
            pltpu.make_async_remote_copy(
                src_ref=src(d, to),
                dst_ref=dst.at[me],
                send_sem=send.at[d],
                recv_sem=recv.at[me],
                device_id=place(to),
                device_id_type=MESH,
            )
        )
    for made in copies:
        made.start()
    return copies


def landed(dst, send, recv, slot, to):
    return pltpu.make_async_remote_copy(
        src_ref=dst.at[slot],
        dst_ref=dst.at[slot],
        send_sem=send.at[0],
        recv_sem=recv.at[slot],
        device_id=to,
        device_id_type=MESH,
    )


def kernel(
    tm, heads, members,
    li_hbm, w_hbm, x_hbm, log_hbm, dy_hbm,
    gx_ref, gl_ref, gi_ref, gw_ref,
    x_ref, dy_ref, log_ref,
    wbuf, libuf, dec, pbuf, bcr, st, sibst, agg, strecv, hin, gout, decay, dgx, lit, grecv, gall, grow,
    w_send, w_recv, li_send, li_recv, d_send, d_recv, p_send, p_recv, s_send, s_recv,
    g_send, g_recv, a_send, a_recv, in_sem,
):
    me = lax.axis_index("tm")
    z = lax.axis_index("heads")
    chips = tm // 2
    span = li_hbm.shape[0]
    heads_here = log_ref.shape[0]
    width = x_ref.shape[1]
    size = width // heads_here
    rows_w = w_hbm.shape[0]
    along = lambda to: (to, z)
    across_z = lambda to: (me, to)
    peer = (lax.rem(me + 1, tm), z)

    loads = [
        pltpu.make_async_copy(src, dst, in_sem.at[k])
        for k, (src, dst) in enumerate((
            (log_hbm, log_ref), (w_hbm, wbuf.at[me]), (x_hbm, x_ref), (dy_hbm, dy_ref),
            (li_hbm, libuf.at[me]),
        ))
    ]
    for made in loads:
        made.start()
    chip, core = me // 2, lax.rem(me, 2)
    barrier = pltpu.get_barrier_semaphore()
    for d in range(1, tm):
        pl.semaphore_signal(
            barrier, inc=1, device_id=along(lax.rem(me + d, tm)), device_id_type=MESH
        )
    for d in range(1, heads):
        pl.semaphore_signal(
            barrier, inc=1, device_id=across_z(lax.rem(z + d, heads)), device_id_type=MESH
        )
        pl.semaphore_signal(
            barrier,
            inc=1,
            device_id=(chip * 2 + 1 - core, lax.rem(z + d, heads)),
            device_id_type=MESH,
        )

    weights = Gather(wbuf, w_send, w_recv, tm, me, z)
    layer = Gather(libuf, li_send, li_recv, tm, me, z)
    started = []

    row = lax.broadcasted_iota(jnp.int32, (span, span), 0)
    col = lax.broadcasted_iota(jnp.int32, (span, span), 1)
    lower = (row >= col).astype(F32)
    upper = (row <= col).astype(F32)
    strict = (row > col).astype(F32)
    head_of = lax.broadcasted_iota(jnp.int32, (heads_here, width), 0) * size
    place = lax.broadcasted_iota(jnp.int32, (heads_here, width), 1)
    spread = ((place >= head_of) & (place < head_of + size)).astype(F32)
    loads[0].wait()
    sums_t = nn(log_ref[...], upper, HIGH)
    sums = sums_t.T
    wide = nn(sums, spread, HIGH)
    total = wide[span - 1 : span, :]
    dec[me] = jnp.broadcast_to(total, (8, width))
    loads[1].wait()
    pl.semaphore_wait(barrier, tm - 1 + 2 * (heads - 1))
    weights.out()
    loads[4].wait()
    layer.share([me])
    started += exchange(lambda d, to: dec.at[me], dec, d_send, d_recv, tm, me, along)
    loads[2].wait()
    loads[3].wait()
    from_start = jnp.exp(wide)
    to_end = jnp.exp(total - wide)
    x = x_ref[...]
    dy = dy_ref[...]
    x_end = to_end * x
    dy_start = from_start * dy
    x_end_t = x_end.T.astype(BF16)
    dy_start_t = dy_start.T.astype(BF16)
    x_end = x_end.astype(BF16)
    dy_start = dy_start.astype(BF16)
    lit[:, :span] = libuf[me].T
    x_half = x.astype(BF16)
    dy_half = dy.astype(BF16)

    dgx_sum = jnp.zeros((span, span), F32)

    def pairs_of(h, so_far):
        cut = slice(h * size, (h + 1) * size)
        gaps = sums_t[h : h + 1, :] - sums[:, h : h + 1]
        step = jnp.where(row <= col, jnp.exp(jnp.minimum(gaps, 0.0)), 0.0)
        pairs = step * nt(x_half[:, cut], dy_half[:, cut])
        decay[h] = step
        dgx[h] = pairs
        return so_far + pairs

    weights.relay()

    sent = []

    def project(slot):
        number = len(sent)
        k = slot // 2
        rows = nn(wbuf[slot], lit[...]).astype(BF16)
        pbuf[k, 0] = rows[:, :span]
        pbuf[k, 1] = rows[:, span:]
        part = lax.rem(k, 2)
        made = []
        for m in range(members):
            to = k // 2 * members + m
            for away in range(2):
                side = core if away == 0 else 1 - core
                made.append((to != z if away == 0 else None, pltpu.make_async_remote_copy(
                    src_ref=pbuf.at[k, away],
                    dst_ref=bcr.at[z, part, core],
                    send_sem=p_send.at[number, 2 * m + away],
                    recv_sem=p_recv.at[z, 2 * part + core],
                    device_id=(chip * 2 + side, to),
                    device_id_type=MESH,
                )))
        sent.append(made)
        for goes, copy in made:
            if goes is None:
                copy.start()
            else:
                pl.when(goes)(copy.start)

    layer.other(chip)
    lit[:, span:] = libuf[chip * 2 + 1 - core].T
    project(me)
    for h in range(heads_here):
        dgx_sum = pairs_of(h, dgx_sum)
    held = weights.near()
    for slot in held:
        project(slot)
    rest = weights.far()
    for slot in rest:
        project(slot)
    layer.first()
    group = z // members
    for part in range(2):
        bcr[z, part, core] = pbuf[2 * group + part, 0]

    def bc_landed(source, place):
        pltpu.make_async_remote_copy(
            src_ref=bcr.at[source, place // 2, lax.rem(place, 2)],
            dst_ref=bcr.at[source, place // 2, lax.rem(place, 2)],
            send_sem=p_send.at[0, 0],
            recv_sem=p_recv.at[source, place],
            device_id=peer,
            device_id_type=MESH,
        ).wait_recv()

    for part in range(2):
        bc_landed(z, 2 * part + 1 - core)
    for d in range(1, heads):
        for k in range(4):
            bc_landed(lax.rem(z + d, heads), k)
    bc = bcr[0].astype(F32)
    for k in range(1, heads):
        bc = bc + bcr[k].astype(F32)
    bc = bc.reshape(2, N, span)
    b_t = bc[0].astype(BF16)
    c_t = bc[1].astype(BF16)

    st[0] = nn(b_t, x_end).astype(BF16)
    st[1] = nn(c_t, dy_start).astype(BF16)
    half = width // 2
    sibling = chip * 2 + 1 - core

    def state_copy(src, dst, to, number, place):
        return pltpu.make_async_remote_copy(
            src_ref=src,
            dst_ref=dst,
            send_sem=s_send.at[number],
            recv_sem=s_recv.at[place],
            device_id=along(to),
            device_id_type=MESH,
        )

    swap = state_copy(st, sibst, sibling, 0, 2 * chip)
    swap.start()
    layer.second(0)
    started.append(swap)
    for d in range(1, tm):
        landed(dec, d_send, d_recv, lax.rem(me + d, tm), peer).wait_recv()
    mine = pl.ds(pl.multiple_of(core * half, half), half)
    own_decay = jnp.exp(dec[me, 0:1, mine])
    sib_decay = jnp.exp(dec[sibling, 0:1, mine])
    one = jnp.ones_like(own_decay)
    first = core == 0
    swap.wait_recv()
    agg[0] = (
        jnp.where(first, sib_decay, one) * st[0, :, mine].astype(F32)
        + jnp.where(first, one, own_decay) * sibst[0, :, mine].astype(F32)
    ).astype(BF16)
    agg[1] = (
        jnp.where(first, one, sib_decay) * st[1, :, mine].astype(F32)
        + jnp.where(first, own_decay, one) * sibst[1, :, mine].astype(F32)
    ).astype(BF16)
    for d in range(1, chips):
        to = lax.rem(chip + d, chips) * 2 + core
        made = state_copy(
            agg.at[(chip + d) // chips], strecv.at[me], to, d, me
        )
        made.start()
        started.append(made)
    b = bc[0].T.astype(BF16)
    c = bc[1].T.astype(BF16)

    cb = nn(b, c_t)
    after = []
    before = []
    for h in range(heads_here):
        cut = slice(h * size, (h + 1) * size)
        weight = decay[h] * cb
        gx_ref[:, cut] = nn(weight.astype(BF16), dy_half[:, cut])
        product = dgx[h] * cb
        after.append(jnp.sum(product, axis=1, keepdims=True))
        before.append(jnp.sum(product, axis=0, keepdims=True))
    before = jnp.concatenate(before, axis=0)
    after = jnp.concatenate(after, axis=1)
    grad_b = nn(c_t, dgx_sum.T.astype(BF16))
    grad_c = nn(b_t, dgx_sum.astype(BF16))
    inside = nn(strict, after, HIGH) - nt(strict, before, HIGH)

    for d in range(1, chips):
        slot = lax.rem(chip + d, chips) * 2 + core
        landed(strecv, s_send, s_recv, slot, peer).wait_recv()
        made = state_copy(strecv.at[slot], strecv.at[slot], sibling, chips - 1 + d, slot)
        made.start()
        started.append(made)
    layer.relay()
    layer.second(1)
    for d in range(1, chips):
        slot = lax.rem(chip + d, chips) * 2 + 1 - core
        landed(strecv, s_send, s_recv, slot, peer).wait_recv()
    hin[...] = jnp.zeros_like(hin)
    gout[...] = jnp.zeros_like(gout)

    def fold(ref, q):
        decays = jnp.exp(dec[2 * q][0:1, :] + dec[2 * q + 1][0:1, :])
        for k in range(2):
            cut = slice(k * half, (k + 1) * half)
            ref[:, cut] = ref[:, cut] * decays[:, cut] + strecv[2 * q + k].astype(F32)

    def forward(q, _):
        fold(hin, q)
        return 0

    def backward(k, _):
        fold(gout, chips - 1 - k)
        return 0

    def fold_sibling(ref, part):
        ref[...] = ref[...] * jnp.exp(dec[sibling][0:1, :]) + sibst[part].astype(F32)

    def send_grad(part, value):
        grecv[z, part] = value.astype(BF16)
        copies = []
        for d in range(1, heads):
            copies.append(pltpu.make_async_remote_copy(
                src_ref=grecv.at[z, part],
                dst_ref=grecv.at[z, part],
                send_sem=g_send.at[d, part],
                recv_sem=g_recv.at[z, part],
                device_id=across_z(lax.rem(z + d, heads)),
                device_id_type=MESH,
            ))
        for made in copies:
            made.start()
        return copies

    lax.fori_loop(0, chips - 1 - chip, backward, 0)
    pl.when(core == 0)(lambda: fold_sibling(gout, 1))
    grad = gout[...]
    grad_half = grad.astype(BF16)
    started += send_grad(0, grad_b + nn(grad_half, x_end_t))
    lax.fori_loop(0, chip, forward, 0)
    pl.when(core == 1)(lambda: fold_sibling(hin, 0))
    state = hin[...]
    state_half = state.astype(BF16)
    started += send_grad(1, grad_c + nn(state_half, dy_start_t))
    weights.share([me] + held + rest)

    from_end = to_end * nn(b, grad_half)
    gx_ref[...] += from_end
    earlier = nt(from_start * nn(c, state_half) * dy, spread, HIGH)
    later = nt(from_end * x, spread, HIGH)
    through = jnp.sum(grad * state, axis=0, keepdims=True) * jnp.exp(total)
    through = nt(jnp.broadcast_to(through, (8, width)), spread, HIGH)
    gl_ref[...] = (
        inside + nn(upper, earlier, HIGH) + nn(strict, later, HIGH) + through[0:1, :]
    ).T

    for d in range(1, heads):
        other = lax.rem(z + d, heads)
        for part in range(2):
            pltpu.make_async_remote_copy(
                src_ref=grecv.at[other, part],
                dst_ref=grecv.at[other, part],
                send_sem=g_send.at[0, 0],
                recv_sem=g_recv.at[other, part],
                device_id=peer,
                device_id_type=MESH,
            ).wait_recv()
    turned = []
    for g in range(heads // members):
        for part in range(2):
            acc = grecv[g * members, part].astype(F32)
            for k in range(1, members):
                acc = acc + grecv[g * members + k, part].astype(F32)
            piece = acc.astype(BF16)
            first = (2 * g + part) * N // rows_w
            for k in range(N // rows_w):
                gall[first + k] = piece[k * rows_w : (k + 1) * rows_w]
            turned.append(piece)
    last = exchange(lambda d, to: gall.at[to], grow, a_send, a_recv, tm, me, along)
    grow[me] = gall[me]
    layer.share(layer.near())
    layer.share(layer.far())
    grad_bc = jnp.concatenate([k.astype(F32).T.astype(BF16) for k in turned], axis=1)
    for made in started:
        made.wait_send()
    for made in sent:
        for goes, copy in made:
            if goes is None:
                copy.wait_send()
            else:
                pl.when(goes)(copy.wait_send)
    for k in range(chips):
        weights.other(k)
    weights.finish()
    gi_ref[...] = nn(grad_bc, wbuf[...].reshape(tm * rows_w, wbuf.shape[2])).astype(BF16)

    for d in range(1, chips):
        layer.other(lax.rem(layer.chip + d, chips))
    for d in range(1, tm):
        landed(grow, a_send, a_recv, lax.rem(me + d, tm), peer).wait_recv()
    rows = jnp.concatenate([grow[k] for k in range(tm)], axis=1)
    gw_ref[...] = nn(rows, libuf[...].reshape(tm * span, libuf.shape[2]))

    for made in last:
        made.wait_send()
    layer.finish()


def store(*refs):
    sems = refs[-1]
    count = (len(refs) - 1) // 2
    copies = [pltpu.make_async_copy(refs[k], refs[count + k], sems.at[k]) for k in range(count)]
    for made in copies:
        made.start()
    for made in copies:
        made.wait()


def solution(mesh):
    tm = mesh.shape["tm"]
    heads = mesh.shape["heads"]
    chips = tm // 2

    def on_device(layer_input, proj_weight, ssd_input, log_decay, out_grad):
        span, depth = layer_input.shape
        rows_w = proj_weight.shape[0]
        heads_here = log_decay.shape[1]
        width = ssd_input.shape[1]
        groups = rows_w * tm // (2 * N)
        members = heads // groups
        copies = 14 if chips == 4 else 4 * (chips - 1) + 2
        dma = lambda *shape: pltpu.SemaphoreType.DMA(shape)
        vmem = pl.BlockSpec(memory_space=pltpu.VMEM)
        hbm = pl.BlockSpec(memory_space=pltpu.HBM)
        shapes = (
            jax.ShapeDtypeStruct((span, width), F32),
            jax.ShapeDtypeStruct((heads_here, span), F32),
            jax.ShapeDtypeStruct((span, depth), BF16),
            jax.ShapeDtypeStruct((rows_w, depth), F32),
        )

        def body(*refs):
            kernel(tm, heads, members, *refs)

        results = pl.pallas_call(
            body,
            out_shape=tuple(pltpu.VMEM(k.shape, k.dtype) for k in shapes),
            in_specs=[hbm] * 5,
            out_specs=(vmem,) * 4,
            scratch_shapes=[
                pltpu.VMEM((span, width), F32),
                pltpu.VMEM((span, width), F32),
                pltpu.VMEM((heads_here, span), F32),
                pltpu.VMEM((tm, rows_w, depth), BF16),
                pltpu.VMEM((tm, span, depth), BF16),
                pltpu.VMEM((tm, 8, width), F32),
                pltpu.VMEM((chips, 2, rows_w, span), BF16),
                pltpu.VMEM((heads, 2, 2, rows_w, span), BF16),
                pltpu.VMEM((2, N, width), BF16),
                pltpu.VMEM((2, N, width), BF16),
                pltpu.VMEM((2, N, width // 2), BF16),
                pltpu.VMEM((tm, N, width // 2), BF16),
                pltpu.VMEM((N, width), F32),
                pltpu.VMEM((N, width), F32),
                pltpu.VMEM((heads_here, span, span), F32),
                pltpu.VMEM((heads_here, span, span), F32),
                pltpu.VMEM((depth, 2 * span), BF16),
                pltpu.VMEM((heads, 2, N, span), BF16),
                pltpu.VMEM((tm, rows_w, span), BF16),
                pltpu.VMEM((tm, rows_w, span), BF16),
                dma(copies), dma(tm, 2),
                dma(copies + chips), dma(tm, 2),
                dma(tm), dma(tm),
                dma(chips, 2 * members), dma(heads, 4),
                dma(tm), dma(tm),
                dma(heads, 2), dma(heads, 2),
                dma(tm), dma(tm),
                dma(5),
            ],
            compiler_params=pltpu.CompilerParams(
                collective_id=0, has_side_effects=True, vmem_limit_bytes=56 * 1024 * 1024
            ),
        )(layer_input, proj_weight, ssd_input, log_decay.T, out_grad)
        grad_x, grad_log, grad_input, grad_weight = pl.pallas_call(
            store,
            out_shape=shapes,
            in_specs=[vmem] * 4,
            out_specs=(hbm,) * 4,
            scratch_shapes=[dma(4)],
            compiler_params=pltpu.CompilerParams(vmem_limit_bytes=1024 * 1024),
        )(*results)
        return grad_x, grad_log.T, grad_input, grad_weight

    return jax.shard_map(
        on_device,
        mesh=mesh,
        in_specs=(P("tm", "heads"),) * 5,
        out_specs=(P("tm", "heads"),) * 4,
        check_vma=False,
    )
```
